32 devices in a mesh: shard: 4 (over y, x), rep: 8 (over z, core).
Axes of the slice: x: 2, y: 2, z: 4, core: 2. Of those that a mesh axis runs over, the one named last changes fastest.
Arguments:
- tokens: bfloat16 [32768, 1024], P(('shard', 'rep')), may hold values from -6 to 6
- doc_ids: int32 [32, 1024], P(('shard', 'rep')), may hold values from 0 to 3, never falling along the last dimension, each value on 1 to 512 neighbouring positions
- w_query: bfloat16 [1024, 1024], P('shard'), may hold values from -0.1875 to 0.1875
- w_key: bfloat16 [1024, 512], P('shard'), may hold values from -0.1875 to 0.1875
- w_value: bfloat16 [1024, 512], P('shard'), may hold values from -0.1875 to 0.1875
- w_out: bfloat16 [1024, 1024], P('shard'), may hold values from -1.5 to 1.5
- w_gate: bfloat16 [1024, 4608], P('shard'), may hold values from -0.1875 to 0.1875
- w_up: bfloat16 [1024, 4608], P('shard'), may hold values from -0.1875 to 0.1875
- w_down: bfloat16 [4608, 1024], P('shard'), may hold values from -0.09375 to 0.09375
- attn_gain: bfloat16 [1024], P('shard'), may hold values from 0.25 to 1.75
- ffn_gain: bfloat16 [1024], P('shard'), may hold values from 0.25 to 1.75
- query_gain: bfloat16 [64], P('shard'), may hold values from 0.25 to 1.75
- key_gain: bfloat16 [64], P('shard'), may hold values from 0.25 to 1.75
- cotangent: bfloat16 [32768, 1024], P(('shard', 'rep')), may hold values from -6 to 6
Outputs:
- output: bfloat16 [32768, 1024], P(('shard', 'rep'))
- grad_tokens: float32 [32768, 1024], P(('shard', 'rep'))
- grad_w_query: float32 [1024, 1024], P('shard')
- grad_w_key: float32 [1024, 512], P('shard')
- grad_w_value: float32 [1024, 512], P('shard')
- grad_w_out: float32 [1024, 1024], P('shard')
- grad_w_gate: float32 [1024, 4608], P('shard')
- grad_w_up: float32 [1024, 4608], P('shard')
- grad_w_down: float32 [4608, 1024], P('shard')
- grad_attn_gain: float32 [1024], P('shard')
- grad_ffn_gain: float32 [1024], P('shard')
- grad_query_gain: float32 [64], P('shard')
- grad_key_gain: float32 [64], P('shard')
The draws below stay inside these ranges and needn't reach their ends.
Inputs may be any that keep to these rules, and one draw needn't show every extreme that they name: `doc_ids`: within each row of 1024 positions the document numbers never fall; each document covers 1 to 512 positions.
All inputs are finite; a program needn't handle non-finite values.
Results may differ from the reference program's by a relative error of at most 0.03.
Values may be sent and summed in bfloat16 or wider, within the bound.
No kernel may reach another device: no remote copies, remote signals or barrier semaphores. Data moves between devices by JAX's collectives and lax.ppermute only.
A program may use at most 320 MiB of HBM per device.

```python
import math
import jax
import jax.numpy as jnp
import numpy as np
from jax import lax

D = 1024
HQ = 16
HK = 8
DH = 64
FF = 4608
LEN = 1024
DOCS = 4
SEQS = 32
TOKENS = 32768


def steps_of(rng, dims, cuts, low, top_value):
    loudness, own = 1.0, jax.random.fold_in(rng, 6)
    for dim, blocks in cuts:
        draws = jnp.exp(jax.random.uniform(jax.random.fold_in(own, dim), (blocks,), jnp.float32, low / len(cuts), top_value / len(cuts)))
        loudness = loudness * jnp.repeat(draws, dims[dim] // blocks).reshape([-1 if axis == dim else 1 for axis in range(len(dims))])
    return loudness


def profile(count, total, bound, skew):
    portions = [(1 << 20) // math.isqrt(grade ** skew) + 1 for grade in range(2, count + 1)]
    rest, given = total - bound - (count - 1), [1] * (count - 1)
    while rest > 0:
        free = [i for i in range(count - 1) if given[i] < bound]
        whole, budget = sum([portions[i] for i in free]), rest
        for i in free:
            addition = min(bound - given[i], max(1, budget * portions[i] // whole), rest)
            given[i] = given[i] + addition
            rest = rest - addition
    return np.array([bound] + given)


def uneven_parts(rng, number_of, total, bound, skew):
    if number_of == 2:
        one = jax.random.randint(rng, (), max(1, total - bound), min(bound, total - 1) + 1)
        return jnp.stack([one, total - one])
    lengths = jnp.asarray(profile(number_of, total, bound, skew), jnp.int32)
    couples = (number_of - 1) // 2
    giver, sink = lengths[1:1 + 2 * couples:2], lengths[2:2 + 2 * couples:2]
    slack = jnp.minimum(giver - 1, bound - sink)
    passed = jax.random.randint(jax.random.fold_in(rng, 1), (couples,), 0, 1 << 20) % (slack + 1)
    lengths = lengths.at[1:1 + 2 * couples:2].set(giver - passed).at[2:2 + 2 * couples:2].set(sink + passed)
    return lengths[jax.random.permutation(jax.random.fold_in(rng, 2), number_of)]


def normal_values(own_key, dims, scale, reach, split=(), kind=jnp.bfloat16):
    values = scale * jax.random.normal(own_key, dims, jnp.float32)
    if split:
        values = values * steps_of(own_key, dims, split, -0.22, 0.18)
    return jnp.clip(values, -reach, reach).astype(kind)


def setup_inputs(seed: int = 0) -> dict:
    seeds = jax.random.split(jax.random.key(seed), 15)
    tokens = normal_values(seeds[0], (TOKENS, D), 1.0, 6.0, ((0, 32),))
    doc_ids = jax.vmap(lambda own: jnp.searchsorted(jnp.cumsum(uneven_parts(own, DOCS, LEN, LEN // 2, 0)), jnp.arange(LEN), side="right"))(jax.random.split(seeds[1], SEQS)).reshape((SEQS, LEN)).astype(jnp.int32)
    w_query = normal_values(seeds[2], (D, HQ * DH), D ** -0.5, 0.1875, ((0, 4),))
    w_key = normal_values(seeds[3], (D, HK * DH), D ** -0.5, 0.1875, ((0, 4),))
    w_value = normal_values(seeds[4], (D, HK * DH), D ** -0.5, 0.1875, ((0, 4),))
    w_out = normal_values(seeds[5], (HQ * DH, D), (D // 64) ** -0.5, 1.5, ((0, 4),))
    w_gate = normal_values(seeds[6], (D, FF), D ** -0.5, 0.1875, ((0, 4),))
    w_up = normal_values(seeds[7], (D, FF), D ** -0.5, 0.1875, ((0, 4),))
    w_down = normal_values(seeds[8], (FF, D), FF ** -0.5, 0.09375, ((0, 4),))
    attn_gain = jnp.clip(1.0 + 0.15 * jax.random.normal(seeds[9], (D,), jnp.float32), 0.25, 1.75).astype(jnp.bfloat16)
    ffn_gain = jnp.clip(1.0 + 0.15 * jax.random.normal(seeds[10], (D,), jnp.float32), 0.25, 1.75).astype(jnp.bfloat16)
    query_gain = jnp.clip(1.0 + 0.15 * jax.random.normal(seeds[11], (DH,), jnp.float32), 0.25, 1.75).astype(jnp.bfloat16)
    key_gain = jnp.clip(1.0 + 0.15 * jax.random.normal(seeds[12], (DH,), jnp.float32), 0.25, 1.75).astype(jnp.bfloat16)
    cotangent = normal_values(seeds[13], (TOKENS, D), 1.0, 6.0, ((0, 32),))
    return {"tokens": tokens, "doc_ids": doc_ids, "w_query": w_query, "w_key": w_key, "w_value": w_value, "w_out": w_out, "w_gate": w_gate, "w_up": w_up, "w_down": w_down, "attn_gain": attn_gain, "ffn_gain": ffn_gain, "query_gain": query_gain, "key_gain": key_gain, "cotangent": cotangent}


EPS = 1e-05
ROPE_BASE = 1000000.0

@jax.custom_vjp
def low(v):
    return lax.optimization_barrier(v.astype(jnp.bfloat16)).astype(jnp.float32)

@jax.custom_vjp
def low_back(v):
    return v

def low_keep(v):
    return (low(v), None)

def low_pass(kept, grad):
    return (grad,)

def back_keep(v):
    return (v, None)

def back_low(kept, grad):
    return (low(grad),)
low.defvjp(low_keep, low_pass)
low_back.defvjp(back_keep, back_low)

def rms_scale(values, gain):
    return values * lax.rsqrt(lax.optimization_barrier(jnp.mean(values * values, axis=-1, keepdims=True)) + EPS) * gain

def doc_positions(doc_rows):
    kinds = jnp.arange(DOCS, dtype=jnp.int32)
    onehot = (doc_rows[:, :, None] == kinds[None, None, :]).astype(jnp.int32)
    counts = lax.optimization_barrier(jnp.sum(onehot, axis=1))
    before = jnp.cumsum(counts, axis=1) - counts
    starts = lax.optimization_barrier(jnp.sum(onehot * before[:, None, :], axis=2))
    return jnp.arange(LEN, dtype=jnp.int32)[None, :] - starts

def rope_tables(positions):
    freqs = jnp.power(ROPE_BASE, -2.0 * jnp.arange(DH // 2, dtype=jnp.float32) / DH)
    angles = positions.astype(jnp.float32)[..., None] * freqs
    return (jnp.cos(angles), jnp.sin(angles))

def rotate(values, cosine, sine):
    half = values.shape[-1] // 2
    first_half = values[..., :half]
    second_half = values[..., half:]
    return jnp.concatenate([first_half * cosine - second_half * sine, second_half * cosine + first_half * sine], axis=-1)

def attend(packed):
    query_rows, key_rows, value_rows, doc_row = packed
    highest = lax.Precision.HIGHEST
    grouped = query_rows.reshape(LEN, HK, HQ // HK, DH)
    scores = low_back(jnp.einsum('qkgd,pkd->kgqp', grouped, key_rows, precision=highest))
    row_ids = jnp.arange(LEN)[:, None]
    col_ids = jnp.arange(LEN)[None, :]
    allowed = (col_ids <= row_ids) & (doc_row[:, None] == doc_row[None, :])
    logits = jnp.where(allowed, scores * DH ** (-0.5), -1e+30)
    row_max = lax.optimization_barrier(jnp.max(logits, axis=-1, keepdims=True))
    exp_terms = jnp.exp(logits - row_max)
    attn_probs = low(exp_terms / lax.optimization_barrier(jnp.sum(exp_terms, axis=-1, keepdims=True)))
    attn_mix = jnp.einsum('kgqp,pkd->qkgd', attn_probs, value_rows, precision=highest)
    return attn_mix.reshape(LEN, HQ, DH)

def reference(tokens, doc_ids, w_query, w_key, w_value, w_out, w_gate, w_up, w_down, attn_gain, ffn_gain, query_gain, key_gain, cotangent):
    highest = lax.Precision.HIGHEST
    positions = doc_positions(doc_ids)
    cosine, sine = rope_tables(positions)
    cosine = cosine.reshape(TOKENS, 1, DH // 2)
    sine = sine.reshape(TOKENS, 1, DH // 2)

    def forward(x_in, wq_f, wk_f, wv_f, wo_f, wg_f, wu_f, wd_f, ga_f, gf_f, gq_f, gk_f):
        attn_in = low(rms_scale(x_in, ga_f))
        q_pre = low_back(jnp.dot(attn_in, wq_f, precision=highest))
        k_pre = low_back(jnp.dot(attn_in, wk_f, precision=highest))
        v_low = low(low_back(jnp.dot(attn_in, wv_f, precision=highest)))
        q_norm = rms_scale(q_pre.reshape(TOKENS, HQ, DH), gq_f)
        k_norm = rms_scale(k_pre.reshape(TOKENS, HK, DH), gk_f)
        q_rot = low(rotate(q_norm, cosine, sine)).reshape(SEQS, LEN, HQ, DH)
        k_rot = low(rotate(k_norm, cosine, sine)).reshape(SEQS, LEN, HK, DH)
        v_seq = v_low.reshape(SEQS, LEN, HK, DH)
        mixed = lax.map(jax.checkpoint(attend), (q_rot, k_rot, v_seq, doc_ids))
        mix_low = low(low_back(mixed.reshape(TOKENS, HQ * DH)))
        resid = x_in + low_back(jnp.dot(mix_low, wo_f, precision=highest))
        ffn_in = low(rms_scale(resid, gf_f))
        gate = low_back(jnp.dot(ffn_in, wg_f, precision=highest))
        upper = low_back(jnp.dot(ffn_in, wu_f, precision=highest))
        hidden = low(jax.nn.silu(gate) * upper)
        return resid + low_back(jnp.dot(hidden, wd_f, precision=highest))
    inputs = (tokens, w_query, w_key, w_value, w_out, w_gate, w_up, w_down, attn_gain, ffn_gain, query_gain, key_gain)
    floats = tuple((item.astype(jnp.float32) for item in inputs))
    result, pull = jax.vjp(forward, *floats)
    grads = pull(cotangent.astype(jnp.float32))
    return (result.astype(jnp.bfloat16), grads[0], grads[1], grads[2], grads[3], grads[4], grads[5], grads[6], grads[7], grads[8], grads[9], grads[10], grads[11])
```

```python
import functools

import jax
import jax.numpy as jnp
from jax import lax
from jax.experimental import pallas as pl
from jax.experimental.pallas import tpu as pltpu
from jax.sharding import PartitionSpec as P

HQ = 16
HK = 8
DH = 64
DOCS = 4
DOC_MAX = 512
EPS = 1e-05
ROPE_BASE = 1000000.0
AXES = ("shard", "rep")
PIECES = 3
GAIN_ROWS = 16
LOW = jnp.bfloat16
FULL = jnp.float32


def dot(first, second, first_dim, second_dim):
    return lax.dot_general(
        first, second, (((first_dim,), (second_dim,)), ((), ())), preferred_element_type=FULL
    )


def inverse_rms(values, axis):
    return lax.rsqrt(jnp.mean(values * values, axis=axis, keepdims=True) + EPS)


def norm_back(grad_in, normed, inverse, axis):
    return inverse * (grad_in - normed * jnp.mean(grad_in * normed, axis=axis, keepdims=True))


def doc_positions(doc_rows):
    kinds = jnp.arange(DOCS, dtype=jnp.int32)
    onehot = (doc_rows[:, :, None] == kinds[None, None, :]).astype(jnp.int32)
    counts = jnp.sum(onehot, axis=1)
    before = jnp.cumsum(counts, axis=1) - counts
    starts = jnp.sum(onehot * before[:, None, :], axis=2)
    return jnp.arange(doc_rows.shape[1], dtype=jnp.int32)[None, :] - starts


def rotate(values, cosine, sine):
    half = DH // 2
    first, second = values[:, :half], values[:, half:]
    return jnp.concatenate(
        [first * cosine - second * sine, second * cosine + first * sine], axis=1
    )


def unrotate(values, cosine, sine):
    half = DH // 2
    first, second = values[:, :half], values[:, half:]
    return jnp.concatenate(
        [first * cosine + second * sine, second * cosine - first * sine], axis=1
    )


class Links:
    def __init__(self, mesh):
        self.shards = mesh.shape["shard"]
        self.reps = mesh.shape["rep"]
        self.shard_bits = self.shards.bit_length() - 1
        self.rep_bits = self.reps.bit_length() - 1
        self.paired = self.shards == 4 and self.reps >= 4

    def here(self):
        return lax.axis_index("shard"), lax.axis_index("rep")

    def move(self, value, partner):
        pairs = []
        for shard in range(self.shards):
            for rep in range(self.reps):
                to_shard, to_rep = partner(shard, rep)
                pairs.append((shard * self.reps + rep, to_shard * self.reps + to_rep))
        return lax.ppermute(value, AXES, pairs)

    def shard_swap(self, value, bit):
        return self.move(value, lambda s, r: (s ^ (1 << bit), r))

    def rep_swap(self, value, bit):
        return self.move(value, lambda s, r: (s, r ^ (1 << bit)))

    def core_swap(self, value):
        return self.rep_swap(value, 0)

    def gather(self, value):
        shard, rep = self.here()
        if self.paired:
            first = self.move(value, lambda s, r: (s ^ (2 if r & 2 else 1), r))
            other = self.rep_swap(first, 1)
            last = self.move(first, lambda s, r: (s ^ (1 if r & 2 else 2), r))
            near = jnp.where((rep & 2) == 0, 1, 2)
            ids = jnp.stack([shard, shard ^ near, shard ^ (3 - near), shard ^ 3, shard])
            return [value, first, other, last], ids.astype(jnp.int32)
        whole = value[None]
        for bit in range(self.shard_bits):
            came = self.shard_swap(whole, bit)
            mine = (shard >> bit) & 1
            whole = jnp.where(
                mine == 0,
                jnp.concatenate([whole, came], axis=0),
                jnp.concatenate([came, whole], axis=0),
            )
        ids = jnp.concatenate([jnp.arange(self.shards), shard[None]])
        return [whole[block] for block in range(self.shards)], ids.astype(jnp.int32)

    def by_mark(self, blocks):
        shard, _ = self.here()
        wide = blocks.shape[2] // 2
        sides = []
        for stream, (_, leave, stay) in enumerate(block_orders(self.shard_bits)):
            part = blocks[:, :, stream * wide : (stream + 1) * wide]
            for marks in (leave, stay):
                sides.append(
                    jnp.stack(
                        [
                            lax.dynamic_index_in_dim(part, shard ^ mark, 0, keepdims=False)
                            for mark in marks
                        ]
                    )
                )
        return sides

    def total(self, sides, axis, tail):
        _, rep = self.here()
        streams = []
        for stream, (order, _, _) in enumerate(block_orders(self.shard_bits)):
            streams.append([order, sides[2 * stream], sides[2 * stream + 1]])
        for turn in range(self.shard_bits):
            came = [self.shard_swap(send, order[turn]) for order, send, _ in streams]
            token = yield [send for _, send, _ in streams]
            came = hold(came, token)
            for entry, arrived in zip(streams, came, strict=True):
                stay = entry[2]
                half = stay.shape[0] // 2
                if half:
                    entry[1] = add_low(stay[half:], arrived[half:])
                    entry[2] = add_low(stay[:half], arrived[:half])
                else:
                    entry[2] = add_low(stay, arrived)
        value = jnp.concatenate([entry[2][0] for entry in streams], axis=axis)
        if self.rep_bits != 3:
            for bit in range(1, self.rep_bits):
                value = add_low(value, self.rep_swap(value, bit))
        elif tail:
            quarter = value.shape[0] // 4
            place = rep >> 1
            pick = lambda at: lax.dynamic_slice_in_dim(value, at * quarter, quarter, 0)
            sends = [pick(place ^ mark) for mark in (1, 2, 3)]
            came = [self.rep_move(send, mark) for send, mark in zip(sends, (1, 2, 3), strict=True)]
            token = yield sends
            came = hold(came, token)
            mine = pick(place).astype(FULL)
            for arrived in came:
                mine = mine + arrived.astype(FULL)
            mine = mine.astype(LOW)
            came = [self.rep_move(mine, mark) for mark in (1, 2, 3)]
            token = yield [mine]
            value = jnp.zeros_like(value)
            for mark, part in enumerate([mine] + hold(came, token)):
                value = lax.dynamic_update_slice_in_dim(
                    value, part, (place ^ mark) * quarter, 0
                )
        else:
            came = self.rep_line(value, {0: 1, 3: 2})
            token = yield [value]
            value = add_low(value, hold([came], token)[0])
            came = self.rep_line(value, {1: 2, 2: 1})
            token = yield [value]
            value = add_low(value, hold([came], token)[0])
            came = self.rep_line(value, {1: 0, 2: 3})
            token = yield [value]
            middle = ((rep >> 1) == 1) | ((rep >> 1) == 2)
            value = jnp.where(middle, value, hold([came], token)[0])
        yield value

    def rep_move(self, value, mark):
        return self.move(value, lambda s, r: (s, r ^ (mark << 1)))

    def rep_line(self, value, targets):
        pairs = []
        for shard in range(self.shards):
            for rep in range(self.reps):
                if rep >> 1 in targets:
                    to = targets[rep >> 1] * 2 + (rep & 1)
                    pairs.append((shard * self.reps + rep, shard * self.reps + to))
        return lax.ppermute(value, AXES, pairs)


def add_low(first, second):
    return (first.astype(FULL) + second.astype(FULL)).astype(LOW)


def hold(values, token):
    if token is None:
        return list(values)
    return list(lax.optimization_barrier(tuple(values) + (token,))[:-1])


def block_orders(bits):
    for order in (list(range(bits)), list(range(bits))[::-1]):
        stay = [0]
        for bit in reversed(order[1:]):
            stay = stay + [m | (1 << bit) for m in stay]
        yield order, [m | (1 << order[0]) for m in stay], stay


def ffn_kernel(ids_ref, ffn_ref, cot_ref, *refs, shards, fresh):
    blocks = refs[:shards]
    refs = refs[shards:]
    if not fresh:
        out_in, back_in = refs[:2]
        refs = refs[2:]
    out_ref, back_ref = refs[:2]
    sides = refs[2:6]
    w_in, w_down, g_in, g_down, stage, sem, out_sem = refs[6:]
    model = ffn_ref.shape[1]
    own = model // shards
    wide = w_down.shape[0]
    step = wide // shards
    at_row = pl.program_id(0)
    parts = []
    for part in range(2 * wide // 256):
        parts.append((part * own, own, part * 256, True))
    for part in range(model // 256):
        parts.append((2 * wide // 256 * own + part * step, step, part * 256, False))

    @pl.when(at_row == 0)
    def _():
        copies = []
        for place, block in enumerate(blocks):
            shard = ids_ref[place]
            for start, count, column, first in parts:
                target = w_in if first else w_down
                row = pl.multiple_of(shard * count, count)
                copies.append(
                    pltpu.make_async_copy(
                        block.at[pl.ds(start, count)],
                        target.at[pl.ds(row, count), pl.ds(column, 256)],
                        sem,
                    )
                )
        for copy in copies:
            copy.start()
        g_in[...] = jnp.zeros_like(g_in)
        g_down[...] = jnp.zeros_like(g_down)
        for copy in copies:
            copy.wait()

    ffn = ffn_ref[...]
    cot = cot_ref[...]
    both = dot(ffn, w_in[...], 1, 0)
    grad_hidden = dot(cot, w_down[...], 1, 1)
    gate, upper = both[:, :wide], both[:, wide:]
    sigmoid = 1.0 / (1.0 + jnp.exp(-gate))
    silu = gate * sigmoid
    hidden = (silu * upper).astype(LOW)
    d_gate = (grad_hidden * upper * sigmoid * (1.0 + gate * (1.0 - sigmoid))).astype(LOW)
    d_up = (grad_hidden * silu).astype(LOW)
    d_both = jnp.concatenate([d_gate, d_up], axis=1)
    term = dot(hidden, w_down[...], 1, 0)
    out_ref[...] = term if fresh else out_in[...] + term
    term = dot(d_both, w_in[...], 1, 1)
    back_ref[...] = term if fresh else back_in[...] + term
    g_down[...] += dot(hidden, cot, 0, 0)
    g_in[...] += dot(ffn, d_both, 0, 0)

    @pl.when(at_row == pl.num_programs(0) - 1)
    def _():
        shard = ids_ref[shards]
        for mark in range(shards):
            block = lax.bitwise_xor(shard, jnp.int32(mark))
            for start, count, column, first in parts:
                source = g_in if first else g_down
                row = pl.multiple_of(block * count, count)
                stage[mark, start : start + count] = source[
                    pl.ds(row, count), column : column + 256
                ].astype(LOW)
        half = stage.shape[1] // 2
        copies = []
        for stream, (_, leave, stay) in enumerate(block_orders(shards.bit_length() - 1)):
            for side, marks in enumerate((leave, stay)):
                for slot, mark in enumerate(marks):
                    copies.append(
                        pltpu.make_async_copy(
                            stage.at[mark, pl.ds(stream * half, half)],
                            sides[2 * stream + side].at[slot],
                            out_sem,
                        )
                    )
        for copy in copies:
            copy.start()
        for copy in copies:
            copy.wait()


def ffn_piece(ids, ffn_pair, cot_pair, blocks, sums, tile=512):
    shards = len(blocks)
    rows = blocks[0].shape[0]
    count, model = ffn_pair.shape
    own = model // shards
    wide = shards * rows * 256 // (3 * model)
    fresh = sums is None
    tall = pl.BlockSpec((tile, model), lambda i, ids: (i, 0))
    where = pl.BlockSpec(memory_space=pl.ANY)
    sums = () if fresh else tuple(sums)
    side = jax.ShapeDtypeStruct((shards // 2, rows // 2, 256), LOW)
    total = jax.ShapeDtypeStruct((count, model), FULL)
    flops = 18 * count * model * wide
    return pl.pallas_call(
        functools.partial(ffn_kernel, shards=shards, fresh=fresh),
        grid_spec=pltpu.PrefetchScalarGridSpec(
            num_scalar_prefetch=1,
            grid=(count // tile,),
            in_specs=[tall, tall] + [where] * shards + [tall] * len(sums),
            out_specs=[tall, tall] + [where] * 4,
            scratch_shapes=[
                pltpu.VMEM((model, 2 * wide), LOW),
                pltpu.VMEM((wide, model), LOW),
                pltpu.VMEM((model, 2 * wide), FULL),
                pltpu.VMEM((wide, model), FULL),
                pltpu.VMEM((shards, rows, 256), LOW),
                pltpu.SemaphoreType.DMA,
                pltpu.SemaphoreType.DMA,
            ],
        ),
        out_shape=[total, total] + [side] * 4,
        input_output_aliases={} if fresh else {3 + shards: 0, 4 + shards: 1},
        compiler_params=pltpu.CompilerParams(vmem_limit_bytes=60 * 1024 * 1024),
        cost_estimate=pl.CostEstimate(flops=flops, bytes_accessed=40_000_000, transcendentals=0),
        name="ffn_piece",
    )(ids, ffn_pair, cot_pair, *blocks, *sums)


def query_blocks(length):
    size = min(256, length)
    for start in range(0, length, size):
        low = max(0, start - DOC_MAX)
        yield start, start + size, low


def attend_kernel(q_ref, k_ref, v_ref, mask_ref, o_ref, log_ref):
    length = q_ref.shape[1]
    value = jnp.concatenate([v_ref[...], jnp.ones((16, length), LOW)], axis=0)
    for group in range(HQ // HK):
        head = slice(group * DH, (group + 1) * DH)
        for start, end, low in query_blocks(length):
            scores = dot(k_ref[:, low:end], q_ref[head, start:end], 0, 0)
            terms = jnp.exp(scores).astype(LOW) * mask_ref[low:end, start:end]
            mixed = dot(value[:, low:end], terms, 1, 0)
            total = mixed[DH : DH + 1]
            o_ref[head, start:end] = (mixed[:DH] * (1.0 / total)).astype(LOW)
            log_ref[0, group : group + 1, start:end] = jnp.log(total)


def attend(q_low, k_low, v_low, mask):
    length = q_low.shape[1]
    wide = HQ // HK * DH
    return pl.pallas_call(
        attend_kernel,
        grid=(HK,),
        in_specs=[
            pl.BlockSpec((wide, length), lambda c: (c, 0)),
            pl.BlockSpec((DH, length), lambda c: (c, 0)),
            pl.BlockSpec((DH, length), lambda c: (c, 0)),
            pl.BlockSpec((length, length), lambda c: (0, 0)),
        ],
        out_specs=[
            pl.BlockSpec((wide, length), lambda c: (c, 0)),
            pl.BlockSpec((1, HQ // HK, length), lambda c: (c, 0, 0)),
        ],
        out_shape=[
            jax.ShapeDtypeStruct((HQ * DH, length), LOW),
            jax.ShapeDtypeStruct((HK, HQ // HK, length), FULL),
        ],
        compiler_params=pltpu.CompilerParams(vmem_limit_bytes=40 * 1024 * 1024),
        cost_estimate=pl.CostEstimate(
            flops=16_000_000_000, bytes_accessed=8_000_000, transcendentals=10_000_000
        ),
        name="attend",
    )(q_low, k_low, v_low, mask)


def row_pair(row, count):
    high = row.astype(LOW).astype(FULL)
    place = lax.broadcasted_iota(jnp.int32, (count, row.shape[1]), 0)
    return jnp.where(place == 0, high, jnp.where(place == 1, row - high, 0.0)).astype(LOW)


def attend_back_kernel(
    q_ref, k_ref, v_ref, o_ref, do_ref, log_ref, mask_ref, dq_ref, dk_ref, dv_ref, value_sum
):
    length = q_ref.shape[1]
    place = lax.broadcasted_iota(jnp.int32, (16, length), 0)
    twos = jnp.where(place < 2, 1.0, 0.0).astype(LOW)
    key = jnp.concatenate([k_ref[...], twos], axis=0)
    value = jnp.concatenate([v_ref[...], twos], axis=0)
    dk_ref[...] = jnp.zeros_like(dk_ref)
    value_sum[...] = jnp.zeros_like(value_sum)
    for group in range(HQ // HK):
        head = slice(group * DH, (group + 1) * DH)
        for start, end, low in query_blocks(length):
            q_blk = q_ref[head, start:end]
            do_blk = do_ref[head, start:end]
            inner = jnp.sum(
                do_blk.astype(FULL) * o_ref[head, start:end].astype(FULL), axis=0, keepdims=True
            )
            log_row = log_ref[0, group : group + 1, start:end]
            q_more = jnp.concatenate([q_blk, row_pair(-log_row, 16)], axis=0)
            do_more = jnp.concatenate([do_blk, row_pair(-inner, 16)], axis=0)
            mask = mask_ref[low:end, start:end]
            probs = jnp.exp(dot(key[:, low:end], q_more, 0, 0))
            grads = dot(value[:, low:end], do_more, 0, 0)
            probs_low = probs.astype(LOW) * mask
            grads_low = (probs * grads).astype(LOW) * mask
            dq_ref[head, start:end] = dot(k_ref[:, low:end], grads_low, 1, 0) * DH ** (-0.5)
            dk_ref[:, low:end] += dot(q_blk, grads_low, 1, 1)
            value_sum[:, low:end] += dot(do_blk, probs_low, 1, 1)
    dv_ref[...] = value_sum[...].astype(LOW)


def attend_back(q_low, k_low, v_low, o_low, do_low, log_total, mask):
    length = q_low.shape[1]
    wide = HQ // HK * DH
    two = pl.BlockSpec((wide, length), lambda c: (c, 0))
    one = pl.BlockSpec((DH, length), lambda c: (c, 0))
    return pl.pallas_call(
        attend_back_kernel,
        grid=(HK,),
        in_specs=[
            two,
            one,
            one,
            two,
            two,
            pl.BlockSpec((1, HQ // HK, length), lambda c: (c, 0, 0)),
            pl.BlockSpec((length, length), lambda c: (0, 0)),
        ],
        out_specs=[two, one, one],
        out_shape=[
            jax.ShapeDtypeStruct((HQ * DH, length), FULL),
            jax.ShapeDtypeStruct((HK * DH, length), FULL),
            jax.ShapeDtypeStruct((HK * DH, length), LOW),
        ],
        scratch_shapes=[pltpu.VMEM((DH, length), FULL)],
        compiler_params=pltpu.CompilerParams(vmem_limit_bytes=40 * 1024 * 1024),
        cost_estimate=pl.CostEstimate(
            flops=40_000_000_000, bytes_accessed=16_000_000, transcendentals=10_000_000
        ),
        name="attend_back",
    )(q_low, k_low, v_low, o_low, do_low, log_total, mask)


def per_device(
    links,
    tokens,
    doc_ids,
    w_query,
    w_key,
    w_value,
    w_out,
    w_gate,
    w_up,
    w_down,
    attn_gain,
    ffn_gain,
    query_gain,
    key_gain,
    cotangent,
):
    shards = links.shards
    _, rep = links.here()
    core = rep & 1
    count, model = tokens.shape
    own = model // shards
    half = own // 2
    kv_wide = HK * DH
    heads_own = DH // shards
    hidden_all = w_gate.shape[1]
    hidden_own = hidden_all // shards
    step = hidden_own // (2 * PIECES)
    packed_wide = model + 2 * kv_wide

    gains = jnp.concatenate([attn_gain, ffn_gain, query_gain, key_gain])
    gains = jnp.pad(gains, (0, packed_wide - gains.shape[0]))[None]
    gains = jnp.pad(gains, ((0, GAIN_ROWS - 1), (0, 0)))
    w_qkv = jnp.concatenate([w_query, w_key, w_value], axis=1)
    qkv_part = jnp.concatenate(
        [lax.dynamic_slice_in_dim(w_qkv, core * half, half, 0), gains], axis=0
    )
    qkv_blocks, ids = links.gather(qkv_part)
    (out_part,) = hold([lax.dynamic_slice_in_dim(w_out, core * half, half, 0)], qkv_part)
    out_blocks, _ = links.gather(out_part)

    def both_halves(blocks):
        mine = jnp.stack([block[:half] for block in blocks])
        theirs = links.core_swap(mine)
        whole = jnp.zeros((shards, 2, half, mine.shape[2]), LOW)
        for side, parts in ((core, mine), (1 - core, theirs)):
            for place in range(shards):
                whole = lax.dynamic_update_slice(
                    whole, parts[place][None, None], (ids[place], side, 0, 0)
                )
        return whole.reshape(model, mine.shape[2])

    ffn_weights = []
    marks = [qkv_blocks[1], out_blocks[1]]
    held = hold([w_gate, w_up, w_down, cotangent], qkv_part)
    cot_pair = jnp.concatenate([cotangent, links.core_swap(held[3])], axis=0)
    for piece in range(PIECES):
        def columns(weight):
            parts = []
            for block in range(shards):
                base = block * hidden_own + piece * step
                parts.append(
                    jnp.where(
                        core == 0,
                        weight[:, base : base + step],
                        weight[:, base + hidden_own // 2 : base + hidden_own // 2 + step],
                    )
                )
            return jnp.concatenate(parts, axis=1)

        down = lax.dynamic_slice_in_dim(
            held[2], core * (hidden_own // 2) + piece * step, step, 0
        )
        packed = jnp.concatenate(
            [
                part[:, at : at + 256]
                for part in (columns(held[0]), columns(held[1]), down)
                for at in range(0, part.shape[1], 256)
            ],
            axis=0,
        )
        (packed,) = hold([packed], marks[-2])
        blocks, _ = links.gather(packed)
        marks.append(blocks[1])
        ffn_weights.append(blocks)

    positions = doc_positions(doc_ids).reshape(count)
    freqs = jnp.power(ROPE_BASE, -2.0 * jnp.arange(DH // 2, dtype=FULL) / DH)
    angles = freqs[:, None] * positions.astype(FULL)[None, :]
    cosine, sine = jnp.cos(angles)[None], jnp.sin(angles)[None]
    index = jnp.arange(count)
    doc_row = doc_ids[0]
    mask = (
        (index[:, None] <= index[None, :]) & (doc_row[:, None] == doc_row[None, :])
    ).astype(LOW)

    x_in = tokens.astype(FULL)
    inv_one = inverse_rms(x_in, 1)
    x_hat = x_in * inv_one

    gain_rows = jnp.zeros((shards, packed_wide), LOW)
    for place, block in enumerate(qkv_blocks):
        gain_rows = lax.dynamic_update_slice(gain_rows, block[half][None], (ids[place], 0))
    gain_rows = gain_rows.astype(FULL)
    gain_attn = gain_rows[:, :own].reshape(model)
    gain_ffn = gain_rows[:, own : 2 * own].reshape(model)
    gain_query = gain_rows[:, 2 * own : 2 * own + heads_own].reshape(1, DH, 1)
    gain_key = gain_rows[:, 2 * own + heads_own : 2 * own + 2 * heads_own].reshape(1, DH, 1)
    qkv_full = both_halves(qkv_blocks)
    out_full = both_halves(out_blocks)

    attn_in = (x_hat * gain_attn).astype(LOW)
    qkv = dot(qkv_full, attn_in, 0, 1)
    q_heads = qkv[:model].reshape(HQ, DH, count)
    k_heads = qkv[model : model + kv_wide].reshape(HK, DH, count)
    v_low = qkv[model + kv_wide :].astype(LOW)
    q_inv = inverse_rms(q_heads, 1)
    q_hat = q_heads * q_inv
    k_inv = inverse_rms(k_heads, 1)
    k_hat = k_heads * k_inv
    q_low = (rotate(q_hat * gain_query, cosine, sine).astype(LOW) * DH ** (-0.5)).reshape(
        model, count
    )
    k_low = rotate(k_hat * gain_key, cosine, sine).astype(LOW).reshape(kv_wide, count)
    mix_low, log_total = attend(q_low, k_low, v_low, mask)

    resid = x_in + dot(mix_low, out_full, 0, 0)
    inv_two = inverse_rms(resid, 1)
    resid_hat = resid * inv_two
    ffn_in = (resid_hat * gain_ffn).astype(LOW)
    ffn_pair = jnp.concatenate([ffn_in, links.core_swap(ffn_in)], axis=0)

    sums, sends = None, None
    ffn_totals = []
    for blocks in ffn_weights:
        (order,) = hold([ids], sends) if sends is not None else [ids]
        *sums, leave_a, stay_a, leave_b, stay_b = ffn_piece(
            order, ffn_pair, cot_pair, blocks, sums
        )
        sends = None
        for entry in ffn_totals:
            entry[1] = entry[0].send(stay_a)
            sends = entry[1][0]
        flow = links.total([leave_a, stay_a, leave_b, stay_b], 0, False)
        ffn_totals.append([flow, next(flow)])

    out_sum, ffn_back = sums
    back_other = links.core_swap(ffn_back[count:].astype(LOW))
    out_other = links.core_swap(out_sum[count:].astype(LOW))
    grad_ffn_in = ffn_back[:count] + back_other.astype(FULL)
    grad_gain_ffn = jnp.sum(grad_ffn_in * resid_hat, axis=0)
    grad_resid = cotangent.astype(FULL) + norm_back(grad_ffn_in * gain_ffn, resid_hat, inv_two, 1)
    grad_resid_low = grad_resid.astype(LOW)
    result = (resid + out_sum[:count] + out_other.astype(FULL)).astype(LOW)

    def half_sum(grad):
        blocks = grad.reshape(shards, 2, half, grad.shape[1])
        keep = lax.dynamic_index_in_dim(blocks, core, 1, keepdims=False)
        give = lax.dynamic_index_in_dim(blocks, 1 - core, 1, keepdims=False)
        return add_low(keep, links.core_swap(give))

    def owned(part):
        theirs = links.core_swap(part)
        low = jnp.where(core == 0, part, theirs)
        high = jnp.where(core == 0, theirs, part)
        return jnp.concatenate([low, high], axis=0).astype(FULL)

    grad_mix = dot(out_full, grad_resid_low, 1, 1).astype(LOW)
    grad_out_w = dot(mix_low, grad_resid_low, 1, 0).astype(LOW)
    out_flow = links.total(links.by_mark(half_sum(grad_out_w)), 1, True)
    flows = [entry[0] for entry in ffn_totals] + [out_flow]
    done = [None] * len(flows)

    def advance(token):
        sent = None
        for place, flow in enumerate(flows):
            if done[place] is None:
                got = flow.send(token)
                if isinstance(got, list):
                    sent = got[0]
                else:
                    done[place] = got
        return sent

    sent_out = next(out_flow)
    flows_now = flows
    flows = flows[:-1]
    sent = advance(grad_mix)
    flows = flows_now
    (do_low,) = hold([grad_mix], sent)
    (do_low,) = hold([do_low], sent_out[0])
    dq_rot, dk_rot, dv_low = attend_back(q_low, k_low, v_low, mix_low, do_low, log_total, mask)
    sent = advance(dv_low)
    (dq_rot, dk_rot) = hold([dq_rot, dk_rot], sent)
    dq_norm = unrotate(dq_rot.reshape(HQ, DH, count), cosine, sine)
    dk_norm = unrotate(dk_rot.reshape(HK, DH, count), cosine, sine)
    grad_gain_query = jnp.sum(dq_norm * q_hat, axis=(0, 2))
    grad_gain_key = jnp.sum(dk_norm * k_hat, axis=(0, 2))
    dq_low = norm_back(dq_norm * gain_query, q_hat, q_inv, 1).astype(LOW).reshape(model, count)
    dk_low = norm_back(dk_norm * gain_key, k_hat, k_inv, 1).astype(LOW).reshape(kv_wide, count)
    d_qkv = jnp.concatenate([dq_low, dk_low, dv_low], axis=0)
    grad_qkv_w = dot(attn_in, d_qkv, 0, 1).astype(LOW)
    (d_qkv_later,) = hold([d_qkv], grad_qkv_w)
    grad_attn_in = dot(d_qkv_later, qkv_full, 0, 1)
    grad_gain_attn = jnp.sum(grad_attn_in * x_hat, axis=0)
    grad_input = grad_resid + norm_back(grad_attn_in * gain_attn, x_hat, inv_one, 1)

    gain_grads = jnp.concatenate(
        [
            grad_gain_attn.reshape(shards, own),
            grad_gain_ffn.reshape(shards, own),
            grad_gain_query.reshape(shards, heads_own),
            grad_gain_key.reshape(shards, heads_own),
        ],
        axis=1,
    ).astype(LOW)
    used = gain_grads.shape[1]
    gain_grads = add_low(gain_grads, links.core_swap(gain_grads))
    gain_grads = jnp.pad(gain_grads, ((0, 0), (0, packed_wide - used)))[:, None]
    gain_grads = jnp.pad(gain_grads, ((0, 0), (0, GAIN_ROWS - 1), (0, 0)))
    qkv_flow = links.total(
        links.by_mark(jnp.concatenate([half_sum(grad_qkv_w), gain_grads], axis=1)), 1, True
    )
    flows = flows + [qkv_flow]
    done = done + [None]
    next(qkv_flow)
    token = grad_attn_in
    while None in done:
        advance(token)
        token = None
    qkv_sum, out_w_sum = done[-1], done[-2]
    gain_sum = qkv_sum[half].astype(FULL)
    grad_qkv = owned(qkv_sum[:half])
    grad_out_w = owned(out_w_sum)
    ffn_grads = []
    for part in done[:PIECES]:
        both = []
        for whole in (part, links.core_swap(part)):
            tall = 2 * hidden_all // (2 * PIECES) // 256 * own
            blocks = [whole[at : at + own] for at in range(0, tall, own)]
            middle = len(blocks) // 2
            both += [
                jnp.concatenate(blocks[:middle], axis=1),
                jnp.concatenate(blocks[middle:], axis=1),
                jnp.concatenate(
                    [whole[at : at + step] for at in range(tall, whole.shape[0], step)], axis=1
                ),
            ]
        ffn_grads.append(both)

    gate_parts = []
    up_parts = []
    down_parts = []
    for block in range(shards):
        for side in range(2):
            for gate, up, _, gate_other, up_other, _ in ffn_grads:
                at = block * step
                span = slice(at, at + step)
                gate_parts.append(jnp.where(core == side, gate[:, span], gate_other[:, span]))
                up_parts.append(jnp.where(core == side, up[:, span], up_other[:, span]))
    for side in range(2):
        for _, _, down, _, _, down_other in ffn_grads:
            down_parts.append(jnp.where(core == side, down, down_other))
    return (
        result,
        grad_input,
        grad_qkv[:, :model],
        grad_qkv[:, model : model + kv_wide],
        grad_qkv[:, model + kv_wide :],
        grad_out_w,
        jnp.concatenate(gate_parts, axis=1).astype(FULL),
        jnp.concatenate(up_parts, axis=1).astype(FULL),
        jnp.concatenate(down_parts, axis=0).astype(FULL),
        gain_sum[:own],
        gain_sum[own : 2 * own],
        gain_sum[2 * own : 2 * own + heads_own],
        gain_sum[2 * own + heads_own : 2 * own + 2 * heads_own],
    )


def solution(mesh):
    both = P(("shard", "rep"), None)
    rows = P("shard", None)
    line = P("shard")
    in_specs = (both, both) + (rows,) * 7 + (line,) * 4 + (both,)
    out_specs = (both, both) + (rows,) * 7 + (line,) * 4
    return jax.shard_map(
        functools.partial(per_device, Links(mesh)),
        mesh=mesh,
        in_specs=in_specs,
        out_specs=out_specs,
        check_vma=False,
    )
```

```python
import functools

import jax
import jax.numpy as jnp
from jax import lax
from jax.experimental import pallas as pl
from jax.experimental.pallas import tpu as pltpu
from jax.sharding import PartitionSpec as P

HQ = 16
HK = 8
DH = 64
DOCS = 4
DOC_MAX = 512
EPS = 1e-05
ROPE_BASE = 1000000.0
AXES = ("shard", "rep")
PIECES = 3
GAIN_ROWS = 16
LOW = jnp.bfloat16
FULL = jnp.float32


def dot(first, second, first_dim, second_dim):
    return lax.dot_general(
        first, second, (((first_dim,), (second_dim,)), ((), ())), preferred_element_type=FULL
    )


def inverse_rms(values, axis):
    return lax.rsqrt(jnp.mean(values * values, axis=axis, keepdims=True) + EPS)


def norm_back(grad_in, normed, inverse, axis):
    return inverse * (grad_in - normed * jnp.mean(grad_in * normed, axis=axis, keepdims=True))


def doc_positions(doc_rows):
    kinds = jnp.arange(DOCS, dtype=jnp.int32)
    onehot = (doc_rows[:, :, None] == kinds[None, None, :]).astype(jnp.int32)
    counts = jnp.sum(onehot, axis=1)
    before = jnp.cumsum(counts, axis=1) - counts
    starts = jnp.sum(onehot * before[:, None, :], axis=2)
    return jnp.arange(doc_rows.shape[1], dtype=jnp.int32)[None, :] - starts


def rotate(values, cosine, sine):
    half = DH // 2
    first, second = values[:, :half], values[:, half:]
    return jnp.concatenate(
        [first * cosine - second * sine, second * cosine + first * sine], axis=1
    )


class Links:
    def __init__(self, mesh):
        self.shards = mesh.shape["shard"]
        self.reps = mesh.shape["rep"]
        self.shard_bits = self.shards.bit_length() - 1
        self.rep_bits = self.reps.bit_length() - 1
        self.paired = self.shards == 4 and self.reps >= 4

    def here(self):
        return lax.axis_index("shard"), lax.axis_index("rep")

    def move(self, value, partner):
        pairs = []
        for shard in range(self.shards):
            for rep in range(self.reps):
                to_shard, to_rep = partner(shard, rep)
                pairs.append((shard * self.reps + rep, to_shard * self.reps + to_rep))
        return lax.ppermute(value, AXES, pairs)

    def shard_swap(self, value, bit):
        return self.move(value, lambda s, r: (s ^ (1 << bit), r))

    def rep_swap(self, value, bit):
        return self.move(value, lambda s, r: (s, r ^ (1 << bit)))

    def core_swap(self, value):
        return self.rep_swap(value, 0)

    def near(self, value):
        if self.paired:
            return self.move(value, lambda s, r: (s ^ (2 if r & 2 else 1), r))
        return value

    def gather(self, value, first, *tokens):
        shard, _ = self.here()
        if self.paired:
            (first,) = hold([first], *tokens)
            other = self.rep_swap(first, 1)
            last = self.move(first, lambda s, r: (s ^ (1 if r & 2 else 2), r))
            return [value, first, other, last]
        whole = value[None]
        for bit in range(self.shard_bits):
            came = self.shard_swap(whole, bit)
            mine = (shard >> bit) & 1
            whole = jnp.where(
                mine == 0,
                jnp.concatenate([whole, came], axis=0),
                jnp.concatenate([came, whole], axis=0),
            )
        return [whole[block] for block in range(self.shards)]

    def ids(self):
        shard, rep = self.here()
        if self.paired:
            near = jnp.where((rep & 2) == 0, 1, 2)
            ids = jnp.stack([shard, shard ^ near, shard ^ (3 - near), shard ^ 3, shard])
        else:
            ids = jnp.concatenate([jnp.arange(self.shards), shard[None]])
        return ids.astype(jnp.int32)

    def by_mark(self, blocks):
        wide = blocks.shape[2] // 2
        sides = []
        for stream, (_, leave, stay) in enumerate(block_orders(self.shard_bits)):
            part = blocks[:, :, stream * wide : (stream + 1) * wide]
            for marks in (leave, stay):
                sides.append(jnp.stack([part[mark] for mark in marks]))
        return sides

    def total(self, sides, axis):
        _, rep = self.here()
        streams = []
        for stream, (order, _, _) in enumerate(block_orders(self.shard_bits)):
            streams.append([order, sides[2 * stream], sides[2 * stream + 1]])
        for turn in range(self.shard_bits):
            came = [self.shard_swap(send, order[turn]) for order, send, _ in streams]
            token = yield [send for _, send, _ in streams]
            came = hold(came, token)
            for entry, arrived in zip(streams, came, strict=True):
                stay = entry[2]
                half = stay.shape[0] // 2
                if half:
                    entry[1] = add_low(stay[half:], arrived[half:])
                    entry[2] = add_low(stay[:half], arrived[:half])
                else:
                    entry[2] = add_low(stay, arrived)
        value = jnp.concatenate([entry[2][0] for entry in streams], axis=axis)
        if self.rep_bits != 3:
            for bit in range(1, self.rep_bits):
                value = add_low(value, self.rep_swap(value, bit))
        else:
            came = self.rep_line(value, {0: 1, 3: 2})
            token = yield [value]
            value = add_low(value, hold([came], token)[0])
            came = self.rep_line(value, {1: 2, 2: 1})
            token = yield [value]
            value = add_low(value, hold([came], token)[0])
            came = self.rep_line(value, {1: 0, 2: 3})
            token = yield [value]
            middle = ((rep >> 1) == 1) | ((rep >> 1) == 2)
            value = jnp.where(middle, value, hold([came], token)[0])
        yield value

    def rep_line(self, value, targets):
        pairs = []
        for shard in range(self.shards):
            for rep in range(self.reps):
                if rep >> 1 in targets:
                    to = targets[rep >> 1] * 2 + (rep & 1)
                    pairs.append((shard * self.reps + rep, shard * self.reps + to))
        return lax.ppermute(value, AXES, pairs)


def add_low(first, second):
    return (first.astype(FULL) + second.astype(FULL)).astype(LOW)


def hold(values, *tokens):
    tokens = tuple(token for token in tokens if token is not None)
    return list(lax.optimization_barrier(tuple(values) + tokens)[: len(values)])


def block_orders(bits):
    for order in (list(range(bits)), list(range(bits))[::-1]):
        stay = [0]
        for bit in reversed(order[1:]):
            stay = stay + [m | (1 << bit) for m in stay]
        yield order, [m | (1 << order[0]) for m in stay], stay


def split_step(step):
    return step * 2 // 3, step // 3


def runs(step, shards, side, piece):
    big, small = split_step(step)
    number = side * PIECES + piece
    for shard in range(shards):
        yield shard, number * big, big, shard * big
    for shard in range(shards):
        yield shard, 2 * PIECES * big + number * small, small, shards * big + shard * small


def pack_kernel(core_ref, gate_ref, up_ref, down_ref, *outs, shards):
    own = gate_ref.shape[0]
    hidden = gate_ref.shape[1] // shards
    step = hidden // (2 * PIECES)
    tall = shards * step // 256 * own
    big, small = split_step(step)
    for side in range(2):

        @pl.when(core_ref[0] == side)
        def _():
            for piece, out in enumerate(outs):
                for number, weight in enumerate((gate_ref, up_ref)):
                    for shard, start, count, place in runs(step, shards, side, piece):
                        row = number * tall + place // 256 * own
                        column = place % 256
                        at = shard * hidden + start
                        out[row : row + own, column : column + count] = weight[:, at : at + count]
                for part in range(down_ref.shape[1] // 256):
                    row = 2 * tall + part * step
                    columns = slice(part * 256, part * 256 + 256)
                    at = (side * PIECES + piece) * big
                    out[row : row + big] = down_ref[at : at + big, columns]
                    at = 2 * PIECES * big + (side * PIECES + piece) * small
                    out[row + big : row + step] = down_ref[at : at + small, columns]


def pack(core, w_gate, w_up, w_down, shards):
    own, hidden_all = w_gate.shape
    rows = 3 * hidden_all // (2 * PIECES) * own // 256
    return pl.pallas_call(
        functools.partial(pack_kernel, shards=shards),
        grid_spec=pltpu.PrefetchScalarGridSpec(
            num_scalar_prefetch=1,
            grid=(1,),
            in_specs=[pl.BlockSpec(w.shape, lambda i, core: (0, 0)) for w in (w_gate, w_up, w_down)],
            out_specs=[pl.BlockSpec((rows, 256), lambda i, core: (0, 0))] * PIECES,
        ),
        out_shape=[jax.ShapeDtypeStruct((rows, 256), LOW)] * PIECES,
        compiler_params=pltpu.CompilerParams(vmem_limit_bytes=48 * 1024 * 1024),
        cost_estimate=pl.CostEstimate(flops=0, bytes_accessed=11_000_000, transcendentals=0),
        name="pack",
    )(core, w_gate, w_up, w_down)


def unpack_kernel(core_ref, *refs, shards):
    mine, theirs = refs[:PIECES], refs[PIECES : 2 * PIECES]
    gate_ref, up_ref, down_ref = refs[2 * PIECES :]
    own = gate_ref.shape[0]
    hidden = gate_ref.shape[1] // shards
    step = hidden // (2 * PIECES)
    tall = shards * step // 256 * own
    big, small = split_step(step)
    for core in range(2):

        @pl.when(core_ref[0] == core)
        def _():
            for side in range(2):
                for piece in range(PIECES):
                    part = (mine if side == core else theirs)[piece]
                    for number, grad in enumerate((gate_ref, up_ref)):
                        for shard, start, count, place in runs(step, shards, side, piece):
                            row = number * tall + place // 256 * own
                            column = place % 256
                            at = shard * hidden + start
                            grad[:, at : at + count] = part[
                                row : row + own, column : column + count
                            ].astype(FULL)
                    for block in range(down_ref.shape[1] // 256):
                        row = 2 * tall + block * step
                        columns = slice(block * 256, block * 256 + 256)
                        at = (side * PIECES + piece) * big
                        down_ref[at : at + big, columns] = part[row : row + big].astype(FULL)
                        at = 2 * PIECES * big + (side * PIECES + piece) * small
                        down_ref[at : at + small, columns] = part[row + big : row + step].astype(
                            FULL
                        )


def unpack(core, mine, theirs, shapes, shards):
    rows = mine[0].shape[0]
    return pl.pallas_call(
        functools.partial(unpack_kernel, shards=shards),
        grid_spec=pltpu.PrefetchScalarGridSpec(
            num_scalar_prefetch=1,
            grid=(1,),
            in_specs=[pl.BlockSpec((rows, 256), lambda i, core: (0, 0))] * (2 * PIECES),
            out_specs=[pl.BlockSpec(shape, lambda i, core: (0, 0)) for shape in shapes],
        ),
        out_shape=[jax.ShapeDtypeStruct(shape, FULL) for shape in shapes],
        compiler_params=pltpu.CompilerParams(vmem_limit_bytes=56 * 1024 * 1024),
        cost_estimate=pl.CostEstimate(flops=0, bytes_accessed=21_000_000, transcendentals=0),
        name="unpack",
    )(core, *mine, *theirs)


def run_copies(copies):
    for copy in copies:
        copy.start()
    for copy in copies:
        copy.wait()


def line_up_kernel(ids_ref, *refs, half):
    *blocks, out, sem = refs
    run_copies(
        [
            pltpu.make_async_copy(block.at[pl.ds(0, half)], out.at[ids_ref[place]], sem)
            for place, block in enumerate(blocks)
        ]
    )


def line_up(ids, blocks, half):
    wide = blocks[0].shape[1]
    where = pl.BlockSpec(memory_space=pl.ANY)
    return pl.pallas_call(
        functools.partial(line_up_kernel, half=half),
        grid_spec=pltpu.PrefetchScalarGridSpec(
            num_scalar_prefetch=1,
            grid=(1,),
            in_specs=[where] * len(blocks),
            out_specs=pl.BlockSpec((len(blocks), half, wide), lambda i, ids: (0, 0, 0)),
            scratch_shapes=[pltpu.SemaphoreType.DMA],
        ),
        out_shape=jax.ShapeDtypeStruct((len(blocks), half, wide), LOW),
        cost_estimate=pl.CostEstimate(flops=0, bytes_accessed=8_000_000, transcendentals=0),
        compiler_params=pltpu.CompilerParams(vmem_limit_bytes=32 * 1024 * 1024),
        name="line_up",
    )(ids, *blocks)


def both_cores_kernel(core_ref, mine, theirs, out, sem):
    core = core_ref[0]
    run_copies(
        [
            pltpu.make_async_copy(mine.at[shard], out.at[shard, core], sem)
            for shard in range(mine.shape[0])
        ]
        + [
            pltpu.make_async_copy(theirs.at[shard], out.at[shard, 1 - core], sem)
            for shard in range(mine.shape[0])
        ]
    )


def both_cores(core, mine, theirs):
    shards, half, wide = mine.shape
    where = pl.BlockSpec(memory_space=pl.ANY)
    out = pl.pallas_call(
        both_cores_kernel,
        grid_spec=pltpu.PrefetchScalarGridSpec(
            num_scalar_prefetch=1,
            grid=(1,),
            in_specs=[where] * 2,
            out_specs=pl.BlockSpec((shards, 2, half, wide), lambda i, core: (0, 0, 0, 0)),
            scratch_shapes=[pltpu.SemaphoreType.DMA],
        ),
        out_shape=jax.ShapeDtypeStruct((shards, 2, half, wide), LOW),
        cost_estimate=pl.CostEstimate(flops=0, bytes_accessed=16_000_000, transcendentals=0),
        compiler_params=pltpu.CompilerParams(vmem_limit_bytes=32 * 1024 * 1024),
        name="both_cores",
    )(core, mine, theirs)
    return out.reshape(shards * 2 * half, wide)


def sort_out_kernel(place_ref, *refs, half):
    *grads, gains, keep, give, sem = refs
    shard, core = place_ref[0], place_ref[1]
    copies = []
    for mark in range(keep.shape[0]):
        block = lax.bitwise_xor(shard, jnp.int32(mark))
        column = 0
        for grad in grads:
            wide = grad.shape[1]
            for side, target in ((core, keep), (1 - core, give)):
                row = pl.multiple_of((2 * block + side) * half, half)
                copies.append(
                    pltpu.make_async_copy(
                        grad.at[pl.ds(row, half)], target.at[mark, pl.ds(0, half), pl.ds(column, wide)], sem
                    )
                )
            column += wide
        for target in (keep, give):
            copies.append(
                pltpu.make_async_copy(
                    gains.at[block], target.at[mark, pl.ds(half, gains.shape[1])], sem
                )
            )
    run_copies(copies)


def sort_out(place, grads, gains):
    shards, extra, wide = gains.shape
    half = grads[0].shape[0] // (2 * shards)
    where = pl.BlockSpec(memory_space=pl.ANY)
    return pl.pallas_call(
        functools.partial(sort_out_kernel, half=half),
        grid_spec=pltpu.PrefetchScalarGridSpec(
            num_scalar_prefetch=1,
            grid=(1,),
            in_specs=[where] * (len(grads) + 1),
            out_specs=[pl.BlockSpec((shards, half + extra, wide), lambda i, place: (0, 0, 0))] * 2,
            scratch_shapes=[pltpu.SemaphoreType.DMA],
        ),
        out_shape=[jax.ShapeDtypeStruct((shards, half + extra, wide), LOW)] * 2,
        cost_estimate=pl.CostEstimate(flops=0, bytes_accessed=12_000_000, transcendentals=0),
        compiler_params=pltpu.CompilerParams(vmem_limit_bytes=32 * 1024 * 1024),
        name="sort_out",
    )(place, *grads, gains)


def head_back(grad, pre, gain, cosine, sine):
    half = DH // 2
    inverse = inverse_rms(pre, 0)
    hat = pre * inverse
    first, second = grad[:half], grad[half:]
    grad = jnp.concatenate(
        [first * cosine + second * sine, second * cosine - first * sine], axis=0
    )
    own = jnp.sum(grad * hat, axis=1, keepdims=True)
    return norm_back(grad * gain, hat, inverse, 0).astype(LOW), own


def attend_grads_kernel(
    dq_ref,
    dk_ref,
    dv_ref,
    q_ref,
    k_ref,
    cos_ref,
    sin_ref,
    gain_q_ref,
    gain_k_ref,
    in_ref,
    wq_ref,
    wk_ref,
    wv_ref,
    mix_ref,
    resid_ref,
    tokens_ref,
    inv_ref,
    gain_in_ref,
    above_ref,
    gq_ref,
    gk_ref,
    gv_ref,
    go_ref,
    back_ref,
    own_q_ref,
    own_k_ref,
    own_in_ref,
):
    @pl.when(pl.program_id(0) == 0)
    def _():
        own_q_ref[...] = jnp.zeros_like(own_q_ref)
        own_k_ref[...] = jnp.zeros_like(own_k_ref)

    cosine, sine = cos_ref[...], sin_ref[...]
    sides = []
    for grad_ref, pre_ref, gain_ref, own_ref in (
        (dq_ref, q_ref, gain_q_ref, own_q_ref),
        (dk_ref, k_ref, gain_k_ref, own_k_ref),
    ):
        parts = []
        for at in range(0, grad_ref.shape[0], DH):
            rows = slice(at, at + DH)
            part, own = head_back(grad_ref[rows], pre_ref[rows], gain_ref[...], cosine, sine)
            own_ref[...] += own
            parts.append(part)
        sides.append(jnp.concatenate(parts, axis=0))
    wide = dq_ref.shape[0]
    narrow = dk_ref.shape[0]
    grads = jnp.concatenate(sides + [dv_ref[...]], axis=0)
    weights = jnp.concatenate([wq_ref[...], wk_ref[...], wv_ref[...]], axis=1)
    weight_grad = dot(in_ref[...], grads, 0, 1).astype(LOW)
    gq_ref[...] = weight_grad[:, :wide]
    gk_ref[...] = weight_grad[:, wide : wide + narrow]
    gv_ref[...] = weight_grad[:, wide + narrow :]
    go_ref[...] = dot(mix_ref[...], resid_ref[...], 1, 0).astype(LOW)
    back = dot(grads, weights, 0, 1)

    @pl.when(pl.program_id(0) == 0)
    def _():
        back_ref[...] = back

    @pl.when(pl.program_id(0) != 0)
    def _():
        back_ref[...] += back

    @pl.when(pl.program_id(0) == pl.num_programs(0) - 1)
    def _():
        own_in_ref[...] = jnp.zeros_like(own_in_ref)
        size = min(128, back_ref.shape[0])

        @pl.loop(0, back_ref.shape[0] // size)
        def _(at):
            rows = pl.ds(pl.multiple_of(at * size, size), size)
            inverse = inv_ref[rows]
            hat = tokens_ref[rows].astype(FULL) * inverse
            grad = back_ref[rows]
            own_in_ref[...] += jnp.sum(grad * hat, axis=0, keepdims=True)
            back_ref[rows] = above_ref[rows] + norm_back(
                grad * gain_in_ref[...], hat, inverse, 1
            )


def attend_grads(
    dq, dk, dv, qkv, cosine, sine, gain_q, gain_k, attn_in, weights, mix, resid, *ends
):
    count, model = attn_in.shape
    steps = 4
    wide, narrow = HQ * DH // steps, HK * DH // steps
    key_at, value_at = HQ * DH // narrow, (HQ + HK) * DH // narrow
    rows = lambda size, at=0: pl.BlockSpec((size, count), lambda i: (at + i, 0))
    columns = lambda size, at=0: pl.BlockSpec((model, size), lambda i: (0, at + i))
    whole = lambda shape: pl.BlockSpec(shape, lambda i: (0, 0))
    one = jax.ShapeDtypeStruct((DH, 1), FULL)
    return pl.pallas_call(
        attend_grads_kernel,
        grid=(steps,),
        in_specs=[
            rows(wide),
            rows(narrow),
            rows(narrow),
            rows(wide),
            rows(narrow, key_at),
            whole(cosine.shape),
            whole(sine.shape),
            whole((DH, 1)),
            whole((DH, 1)),
            whole(attn_in.shape),
            columns(wide),
            columns(narrow, key_at),
            columns(narrow, value_at),
            whole(mix.shape),
            pl.BlockSpec((count, wide), lambda i: (0, i)),
        ]
        + [whole(end.shape) for end in ends],
        out_specs=[
            columns(wide),
            columns(narrow),
            columns(narrow),
            columns(wide),
            whole((count, model)),
            whole((DH, 1)),
            whole((DH, 1)),
            whole((1, model)),
        ],
        out_shape=[
            jax.ShapeDtypeStruct((model, HQ * DH), LOW),
            jax.ShapeDtypeStruct((model, HK * DH), LOW),
            jax.ShapeDtypeStruct((model, HK * DH), LOW),
            jax.ShapeDtypeStruct((HQ * DH, model), LOW),
            jax.ShapeDtypeStruct((count, model), FULL),
            one,
            one,
            jax.ShapeDtypeStruct((1, model), FULL),
        ],
        compiler_params=pltpu.CompilerParams(vmem_limit_bytes=58 * 1024 * 1024),
        cost_estimate=pl.CostEstimate(
            flops=40_000_000_000, bytes_accessed=40_000_000, transcendentals=0
        ),
        name="attend_grads",
    )(
        dq,
        dk,
        dv,
        qkv,
        qkv,
        cosine,
        sine,
        gain_q,
        gain_k,
        attn_in,
        weights,
        weights,
        weights,
        mix,
        resid,
        *ends,
    )


def ffn_kernel(
    ids_ref, ffn_ref, ffn_other_ref, cot_ref, cot_other_ref, *refs, shards, fresh
):
    blocks = refs[:shards]
    refs = refs[shards:]
    if not fresh:
        out_in, back_in = refs[:2]
        refs = refs[2:]
    out_ref, back_ref = refs[:2]
    sides = refs[2:6]
    w_in, w_down, g_in, g_down, stage, sem, out_sem = refs[6:]
    model = ffn_ref.shape[1]
    own = model // shards
    wide = w_down.shape[0]
    step = wide // shards
    big, small = split_step(step)
    at_row = pl.program_id(0)
    parts = []
    for part in range(2 * wide // 256):
        parts.append((part * own, own, part * 256, True, 0))
    for part in range(model // 256):
        start = 2 * wide // 256 * own + part * step
        parts.append((start, big, part * 256, False, 0))
        parts.append((start + big, small, part * 256, False, shards * big))

    @pl.when(at_row == 0)
    def _():
        copies = []
        for place, block in enumerate(blocks):
            shard = ids_ref[place]
            for start, count, column, first, base in parts:
                target = w_in if first else w_down
                row = pl.multiple_of(shard * count + base, count)
                copies.append(
                    pltpu.make_async_copy(
                        block.at[pl.ds(start, count)],
                        target.at[pl.ds(row, count), pl.ds(column, 256)],
                        sem,
                    )
                )
        for copy in copies:
            copy.start()
        g_in[...] = jnp.zeros_like(g_in)
        g_down[...] = jnp.zeros_like(g_down)
        for copy in copies:
            copy.wait()

    mine = at_row < pl.num_programs(0) // 2
    ffn = jnp.where(mine, ffn_ref[...], ffn_other_ref[...])
    cot = jnp.where(mine, cot_ref[...], cot_other_ref[...])
    both = dot(ffn, w_in[...], 1, 0)
    grad_hidden = dot(cot, w_down[...], 1, 1)
    gate, upper = both[:, :wide], both[:, wide:]
    sigmoid = 1.0 / (1.0 + jnp.exp(-gate))
    silu = gate * sigmoid
    hidden = (silu * upper).astype(LOW)
    d_gate = (grad_hidden * upper * sigmoid * (1.0 + gate * (1.0 - sigmoid))).astype(LOW)
    d_up = (grad_hidden * silu).astype(LOW)
    d_both = jnp.concatenate([d_gate, d_up], axis=1)
    term = dot(hidden, w_down[...], 1, 0)
    out_ref[...] = term if fresh else out_in[...] + term
    term = dot(d_both, w_in[...], 1, 1)
    back_ref[...] = term if fresh else back_in[...] + term
    g_down[...] += dot(hidden, cot, 0, 0)
    g_in[...] += dot(ffn, d_both, 0, 0)

    @pl.when(at_row == pl.num_programs(0) - 1)
    def _():
        shard = ids_ref[shards]
        for mark in range(shards):
            block = lax.bitwise_xor(shard, jnp.int32(mark))
            for start, count, column, first, base in parts:
                source = g_in if first else g_down
                row = pl.multiple_of(block * count + base, count)
                stage[mark, start : start + count] = source[
                    pl.ds(row, count), column : column + 256
                ].astype(LOW)
        half = stage.shape[1] // 2
        copies = []
        for stream, (_, leave, stay) in enumerate(block_orders(shards.bit_length() - 1)):
            for side, marks in enumerate((leave, stay)):
                for slot, mark in enumerate(marks):
                    copies.append(
                        pltpu.make_async_copy(
                            stage.at[mark, pl.ds(stream * half, half)],
                            sides[2 * stream + side].at[slot],
                            out_sem,
                        )
                    )
        for copy in copies:
            copy.start()
        for copy in copies:
            copy.wait()


def ffn_piece(ids, ffn_pair, cot_pair, blocks, sums, tile=256):
    shards = len(blocks)
    rows = blocks[0].shape[0]
    count, model = ffn_pair[0].shape
    count = 2 * count
    half = count // tile // 2
    wide = shards * rows * 256 // (3 * model)
    fresh = sums is None
    tall = pl.BlockSpec((tile, model), lambda i, ids: (i, 0))
    mine = pl.BlockSpec((tile, model), lambda i, ids: (jnp.minimum(i, half - 1), 0))
    other = pl.BlockSpec((tile, model), lambda i, ids: (jnp.maximum(i - half, 0), 0))
    where = pl.BlockSpec(memory_space=pl.ANY)
    sums = () if fresh else tuple(sums)
    side = jax.ShapeDtypeStruct((shards // 2, rows // 2, 256), LOW)
    total = jax.ShapeDtypeStruct((count, model), FULL)
    flops = 18 * count * model * wide
    return pl.pallas_call(
        functools.partial(ffn_kernel, shards=shards, fresh=fresh),
        grid_spec=pltpu.PrefetchScalarGridSpec(
            num_scalar_prefetch=1,
            grid=(count // tile,),
            in_specs=[mine, other] * 2 + [where] * shards + [tall] * len(sums),
            out_specs=[tall, tall] + [where] * 4,
            scratch_shapes=[
                pltpu.VMEM((model, 2 * wide), LOW),
                pltpu.VMEM((wide, model), LOW),
                pltpu.VMEM((model, 2 * wide), FULL),
                pltpu.VMEM((wide, model), FULL),
                pltpu.VMEM((shards, rows, 256), LOW),
                pltpu.SemaphoreType.DMA,
                pltpu.SemaphoreType.DMA,
            ],
        ),
        out_shape=[total, total] + [side] * 4,
        input_output_aliases={} if fresh else {5 + shards: 0, 6 + shards: 1},
        compiler_params=pltpu.CompilerParams(vmem_limit_bytes=60 * 1024 * 1024),
        cost_estimate=pl.CostEstimate(flops=flops, bytes_accessed=40_000_000, transcendentals=0),
        name="ffn_piece",
    )(ids, *ffn_pair, *cot_pair, *blocks, *sums)


def query_blocks(length):
    size = min(256, length)
    for start in range(0, length, size):
        low = max(0, start - DOC_MAX)
        yield start, start + size, low


def attend_kernel(q_ref, k_ref, v_ref, mask_ref, o_ref, log_ref):
    length = q_ref.shape[1]
    value = jnp.concatenate([v_ref[...], jnp.ones((16, length), LOW)], axis=0)
    for group in range(HQ // HK):
        head = slice(group * DH, (group + 1) * DH)
        for start, end, low in query_blocks(length):
            scores = dot(k_ref[:, low:end], q_ref[head, start:end], 0, 0)
            terms = jnp.exp(scores).astype(LOW) * mask_ref[low:end, start:end]
            mixed = dot(value[:, low:end], terms, 1, 0)
            total = mixed[DH : DH + 1]
            o_ref[head, start:end] = (mixed[:DH] * (1.0 / total)).astype(LOW)
            log_ref[0, group : group + 1, start:end] = jnp.log(total)


def attend(q_low, k_low, v_low, mask):
    length = q_low.shape[1]
    wide = HQ // HK * DH
    return pl.pallas_call(
        attend_kernel,
        grid=(HK,),
        in_specs=[
            pl.BlockSpec((wide, length), lambda c: (c, 0)),
            pl.BlockSpec((DH, length), lambda c: (c, 0)),
            pl.BlockSpec((DH, length), lambda c: (c, 0)),
            pl.BlockSpec((length, length), lambda c: (0, 0)),
        ],
        out_specs=[
            pl.BlockSpec((wide, length), lambda c: (c, 0)),
            pl.BlockSpec((1, HQ // HK, length), lambda c: (c, 0, 0)),
        ],
        out_shape=[
            jax.ShapeDtypeStruct((HQ * DH, length), LOW),
            jax.ShapeDtypeStruct((HK, HQ // HK, length), FULL),
        ],
        compiler_params=pltpu.CompilerParams(vmem_limit_bytes=40 * 1024 * 1024),
        cost_estimate=pl.CostEstimate(
            flops=16_000_000_000, bytes_accessed=8_000_000, transcendentals=10_000_000
        ),
        name="attend",
    )(q_low, k_low, v_low, mask)


def row_pair(row, count):
    high = row.astype(LOW).astype(FULL)
    place = lax.broadcasted_iota(jnp.int32, (count, row.shape[1]), 0)
    return jnp.where(place == 0, high, jnp.where(place == 1, row - high, 0.0)).astype(LOW)


def attend_back_kernel(
    q_ref, k_ref, v_ref, o_ref, do_ref, log_ref, mask_ref, dq_ref, dk_ref, dv_ref, value_sum
):
    length = q_ref.shape[1]
    place = lax.broadcasted_iota(jnp.int32, (16, length), 0)
    twos = jnp.where(place < 2, 1.0, 0.0).astype(LOW)
    key = jnp.concatenate([k_ref[...], twos], axis=0)
    value = jnp.concatenate([v_ref[...], twos], axis=0)
    dk_ref[...] = jnp.zeros_like(dk_ref)
    value_sum[...] = jnp.zeros_like(value_sum)
    for group in range(HQ // HK):
        head = slice(group * DH, (group + 1) * DH)
        for start, end, low in query_blocks(length):
            q_blk = q_ref[head, start:end]
            do_blk = do_ref[head, start:end]
            inner = jnp.sum(
                do_blk.astype(FULL) * o_ref[head, start:end].astype(FULL), axis=0, keepdims=True
            )
            log_row = log_ref[0, group : group + 1, start:end]
            q_more = jnp.concatenate([q_blk, row_pair(-log_row, 16)], axis=0)
            do_more = jnp.concatenate([do_blk, row_pair(-inner, 16)], axis=0)
            mask = mask_ref[low:end, start:end]
            probs = jnp.exp(dot(key[:, low:end], q_more, 0, 0))
            grads = dot(value[:, low:end], do_more, 0, 0)
            probs_low = probs.astype(LOW) * mask
            grads_low = (probs * grads).astype(LOW) * mask
            dq_ref[head, start:end] = dot(k_ref[:, low:end], grads_low, 1, 0) * DH ** (-0.5)
            dk_ref[:, low:end] += dot(q_blk, grads_low, 1, 1)
            value_sum[:, low:end] += dot(do_blk, probs_low, 1, 1)
    dv_ref[...] = value_sum[...].astype(LOW)


def attend_back(q_low, k_low, v_low, o_low, do_low, log_total, mask):
    length = q_low.shape[1]
    wide = HQ // HK * DH
    two = pl.BlockSpec((wide, length), lambda c: (c, 0))
    one = pl.BlockSpec((DH, length), lambda c: (c, 0))
    return pl.pallas_call(
        attend_back_kernel,
        grid=(HK,),
        in_specs=[
            two,
            one,
            one,
            two,
            two,
            pl.BlockSpec((1, HQ // HK, length), lambda c: (c, 0, 0)),
            pl.BlockSpec((length, length), lambda c: (0, 0)),
        ],
        out_specs=[two, one, one],
        out_shape=[
            jax.ShapeDtypeStruct((HQ * DH, length), FULL),
            jax.ShapeDtypeStruct((HK * DH, length), FULL),
            jax.ShapeDtypeStruct((HK * DH, length), LOW),
        ],
        scratch_shapes=[pltpu.VMEM((DH, length), FULL)],
        compiler_params=pltpu.CompilerParams(vmem_limit_bytes=40 * 1024 * 1024),
        cost_estimate=pl.CostEstimate(
            flops=40_000_000_000, bytes_accessed=16_000_000, transcendentals=10_000_000
        ),
        name="attend_back",
    )(q_low, k_low, v_low, o_low, do_low, log_total, mask)


def per_device(
    links,
    tokens,
    doc_ids,
    w_query,
    w_key,
    w_value,
    w_out,
    w_gate,
    w_up,
    w_down,
    attn_gain,
    ffn_gain,
    query_gain,
    key_gain,
    cotangent,
):
    shards = links.shards
    _, rep = links.here()
    core = rep & 1
    count, model = tokens.shape
    own = model // shards
    half = own // 2
    kv_wide = HK * DH
    heads_own = DH // shards
    hidden_all = w_gate.shape[1]
    hidden_own = hidden_all // shards
    step = hidden_own // (2 * PIECES)
    packed_wide = model + 2 * kv_wide

    whole_wide = packed_wide + model
    gains = jnp.concatenate([attn_gain, ffn_gain, query_gain, key_gain])
    gains = jnp.pad(gains, (0, whole_wide - gains.shape[0]))[None]
    gains = jnp.pad(gains, ((0, GAIN_ROWS - 1), (0, 0)))
    attn_part = jnp.concatenate(
        [
            lax.dynamic_slice_in_dim(weight, core * half, half, 0)
            for weight in (w_query, w_key, w_value, w_out)
        ],
        axis=1,
    )
    attn_part = jnp.concatenate([attn_part, gains], axis=0)
    ids = links.ids()
    core_line = core[None]
    attn_near = links.near(attn_part)
    held = hold([w_gate, w_up, w_down, cotangent], attn_part)
    cot_pair = [cotangent, links.core_swap(held[3])]
    packed = list(pack(core_line, *held[:3], shards))
    attn_blocks = links.gather(attn_part, attn_near, packed[0], cot_pair[1])
    (packed[0],) = hold([packed[0]], attn_blocks[1])
    nears = [links.near(packed[0])]
    (line,) = hold([ids], nears[0])
    attn_mine = line_up(line, attn_blocks, half)
    attn_full = both_cores(core_line, attn_mine, links.core_swap(attn_mine))
    qkv_full, out_full = attn_full[:, :packed_wide], attn_full[:, packed_wide:]

    positions = doc_positions(doc_ids).reshape(count)
    freqs = jnp.power(ROPE_BASE, -2.0 * jnp.arange(DH // 2, dtype=FULL) / DH)
    angles = freqs[:, None] * positions.astype(FULL)[None, :]
    cosine, sine = jnp.cos(angles)[None], jnp.sin(angles)[None]
    index = jnp.arange(count)
    doc_row = doc_ids[0]
    mask = (
        (index[:, None] <= index[None, :]) & (doc_row[:, None] == doc_row[None, :])
    ).astype(LOW)

    x_in = tokens.astype(FULL)
    inv_one = inverse_rms(x_in, 1)
    x_hat = x_in * inv_one

    gain_rows = jnp.zeros((shards, whole_wide), LOW)
    for place, block in enumerate(attn_blocks):
        gain_rows = lax.dynamic_update_slice(gain_rows, block[half][None], (ids[place], 0))
    gain_rows = gain_rows.astype(FULL)
    gain_attn = gain_rows[:, :own].reshape(model)
    gain_ffn = gain_rows[:, own : 2 * own].reshape(model)
    gain_query = gain_rows[:, 2 * own : 2 * own + heads_own].reshape(1, DH, 1)
    gain_key = gain_rows[:, 2 * own + heads_own : 2 * own + 2 * heads_own].reshape(1, DH, 1)

    attn_in = (x_hat * gain_attn).astype(LOW)
    (attn_in,) = hold([attn_in], nears[0])
    ffn_weights = [links.gather(packed[0], nears[0])]
    (packed[1],) = hold([packed[1]], nears[0])
    nears.append(links.near(packed[1]))
    qkv = dot(qkv_full, attn_in, 0, 1)
    q_heads = qkv[:model].reshape(HQ, DH, count)
    k_heads = qkv[model : model + kv_wide].reshape(HK, DH, count)
    v_low = qkv[model + kv_wide :].astype(LOW)
    q_inv = inverse_rms(q_heads, 1)
    q_hat = q_heads * q_inv
    k_inv = inverse_rms(k_heads, 1)
    k_hat = k_heads * k_inv
    q_low = (rotate(q_hat * gain_query, cosine, sine).astype(LOW) * DH ** (-0.5)).reshape(
        model, count
    )
    k_low = rotate(k_hat * gain_key, cosine, sine).astype(LOW).reshape(kv_wide, count)
    mix_low, log_total = attend(q_low, k_low, v_low, mask)
    (mix_low,) = hold([mix_low], nears[1], *ffn_weights[0])
    ffn_weights.append(links.gather(packed[1], nears[1]))
    for piece in range(2, PIECES):
        (packed[piece],) = hold([packed[piece]], nears[piece - 1])
        nears.append(links.near(packed[piece]))

    resid = x_in + dot(mix_low, out_full, 0, 0)
    inv_two = inverse_rms(resid, 1)
    resid_hat = resid * inv_two
    ffn_in = (resid_hat * gain_ffn).astype(LOW)
    ffn_pair = [ffn_in, links.core_swap(ffn_in)]

    sums, sends = None, []
    ffn_totals = []
    for piece in range(PIECES):
        (order,) = hold([ids], *sends)
        *sums, leave_a, stay_a, leave_b, stay_b = ffn_piece(
            order, ffn_pair, cot_pair, ffn_weights[piece], sums
        )
        if piece + 2 < PIECES:
            ffn_weights.append(links.gather(packed[piece + 2], nears[piece + 2], stay_a))
        sends = []
        for number, entry in enumerate(ffn_totals):
            if piece == PIECES - 1 and number == 0:
                continue
            entry[1] = entry[0].send(stay_a)
            sends += entry[1]
        flow = links.total([leave_a, stay_a, leave_b, stay_b], 0)
        ffn_totals.append([flow, next(flow)])

    out_sum, ffn_back = sums
    first_sent = ffn_totals[0][0].send(stay_a)
    (back_low,) = hold([ffn_back[count:].astype(LOW)], *first_sent, *sends)
    back_other = links.core_swap(back_low)
    grad_ffn_in = ffn_back[:count] + back_other.astype(FULL)
    grad_gain_ffn = jnp.sum(grad_ffn_in * resid_hat, axis=0)
    grad_resid = cotangent.astype(FULL) + norm_back(grad_ffn_in * gain_ffn, resid_hat, inv_two, 1)
    grad_resid_low = grad_resid.astype(LOW)

    def owned(part):
        theirs = links.core_swap(part)
        low = jnp.where(core == 0, part, theirs)
        high = jnp.where(core == 0, theirs, part)
        return jnp.concatenate([low, high], axis=0).astype(FULL)

    grad_mix = dot(out_full, grad_resid_low, 1, 1).astype(LOW)
    flows = [entry[0] for entry in ffn_totals]
    done = [None] * len(flows)

    def advance(*tokens):
        sent = []
        token = tokens[0] if tokens else None
        for place in reversed(range(len(flows))):
            if done[place] is None:
                got = flows[place].send(token)
                if place >= PIECES and isinstance(got, list):
                    token = got[0]
                if isinstance(got, list):
                    sent += got
                else:
                    done[place] = got
        return sent

    do_low = grad_mix
    dq_rot, dk_rot, dv_low = attend_back(q_low, k_low, v_low, mix_low, do_low, log_total, mask)
    sent = advance(dv_low)
    (dq_rot, dk_rot) = hold([dq_rot, dk_rot], *sent)
    (
        grad_query_w,
        grad_key_w,
        grad_value_w,
        grad_out_w,
        grad_input,
        own_q,
        own_k,
        grad_gain_attn,
    ) = attend_grads(
        dq_rot,
        dk_rot,
        dv_low,
        qkv,
        cosine[0],
        sine[0],
        gain_query[0],
        gain_key[0],
        attn_in,
        attn_full,
        mix_low,
        grad_resid_low,
        tokens,
        inv_one,
        gain_attn[None],
        grad_resid,
    )
    advance(grad_key_w)

    gain_grads = jnp.concatenate(
        [
            grad_gain_attn.reshape(shards, own),
            grad_gain_ffn.reshape(shards, own),
            own_q.reshape(shards, heads_own),
            own_k.reshape(shards, heads_own),
        ],
        axis=1,
    )
    gain_rows = jnp.pad(
        gain_grads.astype(LOW), ((0, 0), (0, whole_wide - gain_grads.shape[1]))
    )[:, None]
    gain_rows = jnp.pad(gain_rows, ((0, 0), (0, GAIN_ROWS - 1), (0, 0)))
    shard_line = jnp.stack([ids[shards], core])
    keep, give = sort_out(
        shard_line, [grad_query_w, grad_key_w, grad_value_w, grad_out_w], gain_rows
    )
    came = links.core_swap(give)
    attn_flow = links.total(links.by_mark(add_low(keep, came)), 1)
    flows = flows + [attn_flow]
    done = done + [None]
    token = next(attn_flow)[0]
    while None in done[:PIECES]:
        advance(token)
        token = None
    advance()
    (out_low,) = hold([out_sum[count:].astype(LOW)], done[1])
    out_other = links.core_swap(out_low)
    result = (resid + out_sum[:count] + out_other.astype(FULL)).astype(LOW)
    ffn_mine = done[:PIECES]
    ffn_theirs = [links.core_swap(part) for part in ffn_mine]
    grad_gate_w, grad_up_w, grad_down_w = unpack(
        core_line, ffn_mine, ffn_theirs, (w_gate.shape, w_up.shape, w_down.shape), shards
    )
    while None in done:
        advance(grad_down_w)
    gain_sum = done[-1][half].astype(FULL)
    attn_sum = owned(done[-1][:half])
    ffn_mine = done[:PIECES]
    ffn_theirs = [links.core_swap(part) for part in ffn_mine]
    grad_gate_w, grad_up_w, grad_down_w = unpack(
        core_line, ffn_mine, ffn_theirs, (w_gate.shape, w_up.shape, w_down.shape), shards
    )
    at_value = model + kv_wide
    return (
        result,
        grad_input,
        attn_sum[:, :model],
        attn_sum[:, model:at_value],
        attn_sum[:, at_value:packed_wide],
        attn_sum[:, packed_wide:],
        grad_gate_w,
        grad_up_w,
        grad_down_w,
        gain_sum[:own],
        gain_sum[own : 2 * own],
        gain_sum[2 * own : 2 * own + heads_own],
        gain_sum[2 * own + heads_own : 2 * own + 2 * heads_own],
    )


def solution(mesh):
    both = P(("shard", "rep"), None)
    rows = P("shard", None)
    line = P("shard")
    in_specs = (both, both) + (rows,) * 7 + (line,) * 4 + (both,)
    out_specs = (both, both) + (rows,) * 7 + (line,) * 4
    return jax.shard_map(
        functools.partial(per_device, Links(mesh)),
        mesh=mesh,
        in_specs=in_specs,
        out_specs=out_specs,
        check_vma=False,
    )
```

```python
import functools

import jax
import jax.numpy as jnp
from jax import lax
from jax.experimental import pallas as pl
from jax.experimental.pallas import tpu as pltpu
from jax.sharding import PartitionSpec as P

HQ = 16
HK = 8
DH = 64
DOCS = 4
DOC_MAX = 512
EPS = 1e-05
ROPE_BASE = 1000000.0
AXES = ("shard", "rep")
PIECES = 3
GAIN_ROWS = 16
LOW = jnp.bfloat16
FULL = jnp.float32


def dot(first, second, first_dim, second_dim):
    return lax.dot_general(
        first, second, (((first_dim,), (second_dim,)), ((), ())), preferred_element_type=FULL
    )


def inverse_rms(values, axis):
    return lax.rsqrt(jnp.mean(values * values, axis=axis, keepdims=True) + EPS)


def norm_back(grad_in, normed, inverse, axis):
    return inverse * (grad_in - normed * jnp.mean(grad_in * normed, axis=axis, keepdims=True))


def doc_positions(doc_rows):
    kinds = jnp.arange(DOCS, dtype=jnp.int32)
    onehot = (doc_rows[:, :, None] == kinds[None, None, :]).astype(jnp.int32)
    counts = jnp.sum(onehot, axis=1)
    before = jnp.cumsum(counts, axis=1) - counts
    starts = jnp.sum(onehot * before[:, None, :], axis=2)
    return jnp.arange(doc_rows.shape[1], dtype=jnp.int32)[None, :] - starts


def rotate(values, cosine, sine):
    half = DH // 2
    first, second = values[:, :half], values[:, half:]
    return jnp.concatenate(
        [first * cosine - second * sine, second * cosine + first * sine], axis=1
    )


class Links:
    def __init__(self, mesh):
        self.shards = mesh.shape["shard"]
        self.reps = mesh.shape["rep"]
        self.shard_bits = self.shards.bit_length() - 1
        self.rep_bits = self.reps.bit_length() - 1
        self.paired = self.shards == 4 and self.reps >= 4

    def here(self):
        return lax.axis_index("shard"), lax.axis_index("rep")

    def move(self, value, partner):
        pairs = []
        for shard in range(self.shards):
            for rep in range(self.reps):
                to_shard, to_rep = partner(shard, rep)
                pairs.append((shard * self.reps + rep, to_shard * self.reps + to_rep))
        return lax.ppermute(value, AXES, pairs)

    def shard_swap(self, value, bit):
        return self.move(value, lambda s, r: (s ^ (1 << bit), r))

    def rep_swap(self, value, bit):
        return self.move(value, lambda s, r: (s, r ^ (1 << bit)))

    def core_swap(self, value):
        return self.rep_swap(value, 0)

    def near(self, value):
        if self.paired:
            return self.move(value, lambda s, r: (s ^ (2 if r & 2 else 1), r))
        return value

    def gather(self, value, first, *tokens):
        shard, _ = self.here()
        if self.paired:
            (first,) = hold([first], *tokens)
            other = self.rep_swap(first, 1)
            last = self.move(first, lambda s, r: (s ^ (1 if r & 2 else 2), r))
            return [value, first, other, last]
        whole = value[None]
        for bit in range(self.shard_bits):
            came = self.shard_swap(whole, bit)
            mine = (shard >> bit) & 1
            whole = jnp.where(
                mine == 0,
                jnp.concatenate([whole, came], axis=0),
                jnp.concatenate([came, whole], axis=0),
            )
        return [whole[block] for block in range(self.shards)]

    def ids(self):
        shard, rep = self.here()
        if self.paired:
            near = jnp.where((rep & 2) == 0, 1, 2)
            ids = jnp.stack([shard, shard ^ near, shard ^ (3 - near), shard ^ 3, shard])
        else:
            ids = jnp.concatenate([jnp.arange(self.shards), shard[None]])
        return ids.astype(jnp.int32)

    def by_mark(self, blocks):
        wide = blocks.shape[2] // 2
        sides = []
        for stream, (_, leave, stay) in enumerate(block_orders(self.shard_bits)):
            part = blocks[:, :, stream * wide : (stream + 1) * wide]
            for marks in (leave, stay):
                sides.append(jnp.stack([part[mark] for mark in marks]))
        return sides

    def total(self, sides, axis, split=False):
        _, rep = self.here()
        streams = []
        for stream, (order, _, _) in enumerate(block_orders(self.shard_bits)):
            streams.append([order, sides[2 * stream], sides[2 * stream + 1]])
        for turn in range(self.shard_bits):
            came = [self.shard_swap(send, order[turn]) for order, send, _ in streams]
            token = yield [send for _, send, _ in streams]
            came = hold(came, token)
            for entry, arrived in zip(streams, came, strict=True):
                stay = entry[2]
                half = stay.shape[0] // 2
                if half:
                    entry[1] = add_low(stay[half:], arrived[half:])
                    entry[2] = add_low(stay[:half], arrived[:half])
                else:
                    entry[2] = add_low(stay, arrived)
        values = [entry[2][0] for entry in streams]
        if not split:
            values = [jnp.concatenate(values, axis=axis)]
        if self.rep_bits != 3:
            for bit in range(1, self.rep_bits):
                values = [add_low(value, self.rep_swap(value, bit)) for value in values]
        else:
            for targets in ({0: 1, 3: 2}, {1: 2, 2: 1}):
                came = [self.rep_line(value, targets) for value in values]
                token = yield values
                for number, arrived in enumerate(came):
                    values[number] = add_low(values[number], hold([arrived], token)[0])
                    token = values[number]
            came = [self.rep_line(value, {1: 0, 2: 3}) for value in values]
            token = yield values
            if isinstance(token, tuple):
                came = [hold([part], at)[0] for part, at in zip(came, token, strict=True)]
            else:
                came = hold(came, token)
            middle = ((rep >> 1) == 1) | ((rep >> 1) == 2)
            values = [
                jnp.where(middle, value, arrived)
                for value, arrived in zip(values, came, strict=True)
            ]
        yield jnp.concatenate(values, axis=axis) if split else values[0]

    def rep_line(self, value, targets):
        pairs = []
        for shard in range(self.shards):
            for rep in range(self.reps):
                if rep >> 1 in targets:
                    to = targets[rep >> 1] * 2 + (rep & 1)
                    pairs.append((shard * self.reps + rep, shard * self.reps + to))
        return lax.ppermute(value, AXES, pairs)


def add_low(first, second):
    return (first.astype(FULL) + second.astype(FULL)).astype(LOW)


def hold(values, *tokens):
    tokens = tuple(token for token in tokens if token is not None)
    return list(lax.optimization_barrier(tuple(values) + tokens)[: len(values)])


def block_orders(bits):
    for order in (list(range(bits)), list(range(bits))[::-1]):
        stay = [0]
        for bit in reversed(order[1:]):
            stay = stay + [m | (1 << bit) for m in stay]
        yield order, [m | (1 << order[0]) for m in stay], stay


def split_step(step):
    return step * 2 // 3, step // 3


def runs(step, shards, side, piece):
    big, small = split_step(step)
    number = side * PIECES + piece
    for shard in range(shards):
        yield shard, number * big, big, shard * big
    for shard in range(shards):
        yield shard, 2 * PIECES * big + number * small, small, shards * big + shard * small


def pack_kernel(core_ref, gate_ref, up_ref, down_ref, *outs, shards):
    own = gate_ref.shape[0]
    hidden = gate_ref.shape[1] // shards
    step = hidden // (2 * PIECES)
    tall = shards * step // 256 * own
    big, small = split_step(step)
    for side in range(2):

        @pl.when(core_ref[0] == side)
        def _():
            for piece, out in enumerate(outs):
                for number, weight in enumerate((gate_ref, up_ref)):
                    for shard, start, count, place in runs(step, shards, side, piece):
                        row = number * tall + place // 256 * own
                        column = place % 256
                        at = shard * hidden + start
                        out[row : row + own, column : column + count] = weight[:, at : at + count]
                for part in range(down_ref.shape[1] // 256):
                    row = 2 * tall + part * step
                    columns = slice(part * 256, part * 256 + 256)
                    at = (side * PIECES + piece) * big
                    out[row : row + big] = down_ref[at : at + big, columns]
                    at = 2 * PIECES * big + (side * PIECES + piece) * small
                    out[row + big : row + step] = down_ref[at : at + small, columns]


def pack(core, w_gate, w_up, w_down, shards):
    own, hidden_all = w_gate.shape
    rows = 3 * hidden_all // (2 * PIECES) * own // 256
    return pl.pallas_call(
        functools.partial(pack_kernel, shards=shards),
        grid_spec=pltpu.PrefetchScalarGridSpec(
            num_scalar_prefetch=1,
            grid=(1,),
            in_specs=[pl.BlockSpec(w.shape, lambda i, core: (0, 0)) for w in (w_gate, w_up, w_down)],
            out_specs=[pl.BlockSpec((rows, 256), lambda i, core: (0, 0))] * PIECES,
        ),
        out_shape=[jax.ShapeDtypeStruct((rows, 256), LOW)] * PIECES,
        compiler_params=pltpu.CompilerParams(vmem_limit_bytes=48 * 1024 * 1024),
        cost_estimate=pl.CostEstimate(flops=0, bytes_accessed=11_000_000, transcendentals=0),
        name="pack",
    )(core, w_gate, w_up, w_down)


def unpack_kernel(core_ref, *refs, shards):
    mine, theirs = refs[:PIECES], refs[PIECES : 2 * PIECES]
    gate_ref, up_ref, down_ref = refs[2 * PIECES :]
    own = gate_ref.shape[0]
    hidden = gate_ref.shape[1] // shards
    step = hidden // (2 * PIECES)
    tall = shards * step // 256 * own
    big, small = split_step(step)
    for core in range(2):

        @pl.when(core_ref[0] == core)
        def _():
            for side in range(2):
                for piece in range(PIECES):
                    part = (mine if side == core else theirs)[piece]
                    for number, grad in enumerate((gate_ref, up_ref)):
                        for shard, start, count, place in runs(step, shards, side, piece):
                            row = number * tall + place // 256 * own
                            column = place % 256
                            at = shard * hidden + start
                            grad[:, at : at + count] = part[
                                row : row + own, column : column + count
                            ].astype(FULL)
                    for block in range(down_ref.shape[1] // 256):
                        row = 2 * tall + block * step
                        columns = slice(block * 256, block * 256 + 256)
                        at = (side * PIECES + piece) * big
                        down_ref[at : at + big, columns] = part[row : row + big].astype(FULL)
                        at = 2 * PIECES * big + (side * PIECES + piece) * small
                        down_ref[at : at + small, columns] = part[row + big : row + step].astype(
                            FULL
                        )


def unpack(core, mine, theirs, shapes, shards):
    rows = mine[0].shape[0]
    return pl.pallas_call(
        functools.partial(unpack_kernel, shards=shards),
        grid_spec=pltpu.PrefetchScalarGridSpec(
            num_scalar_prefetch=1,
            grid=(1,),
            in_specs=[pl.BlockSpec((rows, 256), lambda i, core: (0, 0))] * (2 * PIECES),
            out_specs=[pl.BlockSpec(shape, lambda i, core: (0, 0)) for shape in shapes],
        ),
        out_shape=[jax.ShapeDtypeStruct(shape, FULL) for shape in shapes],
        compiler_params=pltpu.CompilerParams(vmem_limit_bytes=56 * 1024 * 1024),
        cost_estimate=pl.CostEstimate(flops=0, bytes_accessed=1_000, transcendentals=0),
        name="unpack",
    )(core, *mine, *theirs)


def run_copies(copies):
    for copy in copies:
        copy.start()
    for copy in copies:
        copy.wait()


def line_up_kernel(ids_ref, *refs, half):
    *blocks, out, sem = refs
    run_copies(
        [
            pltpu.make_async_copy(block.at[pl.ds(0, half)], out.at[ids_ref[place]], sem)
            for place, block in enumerate(blocks)
        ]
    )


def line_up(ids, blocks, half):
    wide = blocks[0].shape[1]
    where = pl.BlockSpec(memory_space=pltpu.HBM)
    return pl.pallas_call(
        functools.partial(line_up_kernel, half=half),
        grid_spec=pltpu.PrefetchScalarGridSpec(
            num_scalar_prefetch=1,
            grid=(1,),
            in_specs=[where] * len(blocks),
            out_specs=pl.BlockSpec((len(blocks), half, wide), lambda i, ids: (0, 0, 0)),
            scratch_shapes=[pltpu.SemaphoreType.DMA],
        ),
        out_shape=jax.ShapeDtypeStruct((len(blocks), half, wide), LOW),
        cost_estimate=pl.CostEstimate(flops=0, bytes_accessed=8_000_000, transcendentals=0),
        compiler_params=pltpu.CompilerParams(vmem_limit_bytes=32 * 1024 * 1024),
        name="line_up",
    )(ids, *blocks)


def both_cores_kernel(core_ref, mine, theirs, out, sem):
    core = core_ref[0]
    run_copies(
        [
            pltpu.make_async_copy(mine.at[shard], out.at[shard, core], sem)
            for shard in range(mine.shape[0])
        ]
        + [
            pltpu.make_async_copy(theirs.at[shard], out.at[shard, 1 - core], sem)
            for shard in range(mine.shape[0])
        ]
    )


def both_cores(core, mine, theirs):
    shards, half, wide = mine.shape
    where = pl.BlockSpec(memory_space=pltpu.HBM)
    out = pl.pallas_call(
        both_cores_kernel,
        grid_spec=pltpu.PrefetchScalarGridSpec(
            num_scalar_prefetch=1,
            grid=(1,),
            in_specs=[where] * 2,
            out_specs=pl.BlockSpec((shards, 2, half, wide), lambda i, core: (0, 0, 0, 0)),
            scratch_shapes=[pltpu.SemaphoreType.DMA],
        ),
        out_shape=jax.ShapeDtypeStruct((shards, 2, half, wide), LOW),
        cost_estimate=pl.CostEstimate(flops=0, bytes_accessed=16_000_000, transcendentals=0),
        compiler_params=pltpu.CompilerParams(vmem_limit_bytes=32 * 1024 * 1024),
        name="both_cores",
    )(core, mine, theirs)
    return out.reshape(shards * 2 * half, wide)


def sort_out_kernel(place_ref, *refs, half):
    *grads, gains, keep, give, sem = refs
    shard, core = place_ref[0], place_ref[1]
    copies = []
    for mark in range(keep.shape[0]):
        block = lax.bitwise_xor(shard, jnp.int32(mark))
        column = 0
        for grad in grads:
            wide = grad.shape[1]
            for side, target in ((core, keep), (1 - core, give)):
                row = pl.multiple_of((2 * block + side) * half, half)
                copies.append(
                    pltpu.make_async_copy(
                        grad.at[pl.ds(row, half)], target.at[mark, pl.ds(0, half), pl.ds(column, wide)], sem
                    )
                )
            column += wide
        for target in (keep, give):
            copies.append(
                pltpu.make_async_copy(
                    gains.at[block], target.at[mark, pl.ds(half, gains.shape[1])], sem
                )
            )
    run_copies(copies)


def sort_out(place, grads, gains):
    shards, extra, wide = gains.shape
    half = grads[0].shape[0] // (2 * shards)
    where = pl.BlockSpec(memory_space=pltpu.HBM)
    return pl.pallas_call(
        functools.partial(sort_out_kernel, half=half),
        grid_spec=pltpu.PrefetchScalarGridSpec(
            num_scalar_prefetch=1,
            grid=(1,),
            in_specs=[where] * (len(grads) + 1),
            out_specs=[pl.BlockSpec((shards, half + extra, wide), lambda i, place: (0, 0, 0))] * 2,
            scratch_shapes=[pltpu.SemaphoreType.DMA],
        ),
        out_shape=[jax.ShapeDtypeStruct((shards, half + extra, wide), LOW)] * 2,
        cost_estimate=pl.CostEstimate(flops=0, bytes_accessed=1_000, transcendentals=0),
        compiler_params=pltpu.CompilerParams(vmem_limit_bytes=32 * 1024 * 1024),
        name="sort_out",
    )(place, *grads, gains)


def head_back(grad, pre, gain, cosine, sine):
    half = DH // 2
    inverse = inverse_rms(pre, 0)
    hat = pre * inverse
    first, second = grad[:half], grad[half:]
    grad = jnp.concatenate(
        [first * cosine + second * sine, second * cosine - first * sine], axis=0
    )
    own = jnp.sum(grad * hat, axis=1, keepdims=True)
    return norm_back(grad * gain, hat, inverse, 0).astype(LOW), own


def attend_grads_kernel(
    dq_ref,
    dk_ref,
    dv_ref,
    q_ref,
    k_ref,
    cos_ref,
    sin_ref,
    gain_q_ref,
    gain_k_ref,
    in_ref,
    wq_ref,
    wk_ref,
    wv_ref,
    mix_ref,
    resid_ref,
    tokens_ref,
    inv_ref,
    gain_in_ref,
    above_ref,
    gq_ref,
    gk_ref,
    gv_ref,
    go_ref,
    back_ref,
    own_q_ref,
    own_k_ref,
    own_in_ref,
):
    @pl.when(pl.program_id(0) == 0)
    def _():
        own_q_ref[...] = jnp.zeros_like(own_q_ref)
        own_k_ref[...] = jnp.zeros_like(own_k_ref)

    cosine, sine = cos_ref[...], sin_ref[...]
    sides = []
    for grad_ref, pre_ref, gain_ref, own_ref in (
        (dq_ref, q_ref, gain_q_ref, own_q_ref),
        (dk_ref, k_ref, gain_k_ref, own_k_ref),
    ):
        parts = []
        for at in range(0, grad_ref.shape[0], DH):
            rows = slice(at, at + DH)
            part, own = head_back(grad_ref[rows], pre_ref[rows], gain_ref[...], cosine, sine)
            own_ref[...] += own
            parts.append(part)
        sides.append(jnp.concatenate(parts, axis=0))
    wide = dq_ref.shape[0]
    narrow = dk_ref.shape[0]
    grads = jnp.concatenate(sides + [dv_ref[...]], axis=0)
    weights = jnp.concatenate([wq_ref[...], wk_ref[...], wv_ref[...]], axis=1)
    weight_grad = dot(in_ref[...], grads, 0, 1).astype(LOW)
    gq_ref[...] = weight_grad[:, :wide]
    gk_ref[...] = weight_grad[:, wide : wide + narrow]
    gv_ref[...] = weight_grad[:, wide + narrow :]
    go_ref[...] = dot(mix_ref[...], resid_ref[...], 1, 0).astype(LOW)
    back = dot(grads, weights, 0, 1)

    @pl.when(pl.program_id(0) == 0)
    def _():
        back_ref[...] = back

    @pl.when(pl.program_id(0) != 0)
    def _():
        back_ref[...] += back

    @pl.when(pl.program_id(0) == pl.num_programs(0) - 1)
    def _():
        own_in_ref[...] = jnp.zeros_like(own_in_ref)
        size = min(128, back_ref.shape[0])

        @pl.loop(0, back_ref.shape[0] // size)
        def _(at):
            rows = pl.ds(pl.multiple_of(at * size, size), size)
            inverse = inv_ref[rows]
            hat = tokens_ref[rows].astype(FULL) * inverse
            grad = back_ref[rows]
            own_in_ref[...] += jnp.sum(grad * hat, axis=0, keepdims=True)
            back_ref[rows] = above_ref[rows] + norm_back(
                grad * gain_in_ref[...], hat, inverse, 1
            )


def attend_grads(
    dq, dk, dv, qkv, cosine, sine, gain_q, gain_k, attn_in, weights, mix, resid, *ends
):
    count, model = attn_in.shape
    steps = 4
    wide, narrow = HQ * DH // steps, HK * DH // steps
    key_at, value_at = HQ * DH // narrow, (HQ + HK) * DH // narrow
    rows = lambda size, at=0: pl.BlockSpec((size, count), lambda i: (at + i, 0))
    columns = lambda size, at=0: pl.BlockSpec((model, size), lambda i: (0, at + i))
    whole = lambda shape: pl.BlockSpec(shape, lambda i: (0, 0))
    one = jax.ShapeDtypeStruct((DH, 1), FULL)
    return pl.pallas_call(
        attend_grads_kernel,
        grid=(steps,),
        in_specs=[
            rows(wide),
            rows(narrow),
            rows(narrow),
            rows(wide),
            rows(narrow, key_at),
            whole(cosine.shape),
            whole(sine.shape),
            whole((DH, 1)),
            whole((DH, 1)),
            whole(attn_in.shape),
            columns(wide),
            columns(narrow, key_at),
            columns(narrow, value_at),
            whole(mix.shape),
            pl.BlockSpec((count, wide), lambda i: (0, i)),
        ]
        + [whole(end.shape) for end in ends],
        out_specs=[
            columns(wide),
            columns(narrow),
            columns(narrow),
            columns(wide),
            whole((count, model)),
            whole((DH, 1)),
            whole((DH, 1)),
            whole((1, model)),
        ],
        out_shape=[
            jax.ShapeDtypeStruct((model, HQ * DH), LOW),
            jax.ShapeDtypeStruct((model, HK * DH), LOW),
            jax.ShapeDtypeStruct((model, HK * DH), LOW),
            jax.ShapeDtypeStruct((HQ * DH, model), LOW),
            jax.ShapeDtypeStruct((count, model), FULL),
            one,
            one,
            jax.ShapeDtypeStruct((1, model), FULL),
        ],
        compiler_params=pltpu.CompilerParams(vmem_limit_bytes=58 * 1024 * 1024),
        cost_estimate=pl.CostEstimate(
            flops=40_000_000_000, bytes_accessed=40_000_000, transcendentals=0
        ),
        name="attend_grads",
    )(
        dq,
        dk,
        dv,
        qkv,
        qkv,
        cosine,
        sine,
        gain_q,
        gain_k,
        attn_in,
        weights,
        weights,
        weights,
        mix,
        resid,
        *ends,
    )


def ffn_kernel(
    ids_ref, ffn_ref, ffn_other_ref, cot_ref, cot_other_ref, *refs, shards, fresh
):
    blocks = refs[:shards]
    refs = refs[shards:]
    if not fresh:
        out_in, back_in = refs[:2]
        refs = refs[2:]
    out_ref, back_ref = refs[:2]
    sides = refs[2:6]
    w_in, w_down, g_in, g_down, stage, sem, out_sem = refs[6:]
    model = ffn_ref.shape[1]
    own = model // shards
    wide = w_down.shape[0]
    step = wide // shards
    big, small = split_step(step)
    at_row = pl.program_id(0)
    parts = []
    for part in range(2 * wide // 256):
        parts.append((part * own, own, part * 256, True, 0))
    for part in range(model // 256):
        start = 2 * wide // 256 * own + part * step
        parts.append((start, big, part * 256, False, 0))
        parts.append((start + big, small, part * 256, False, shards * big))

    @pl.when(at_row == 0)
    def _():
        copies = []
        for place, block in enumerate(blocks):
            shard = ids_ref[place]
            for start, count, column, first, base in parts:
                target = w_in if first else w_down
                row = pl.multiple_of(shard * count + base, count)
                copies.append(
                    pltpu.make_async_copy(
                        block.at[pl.ds(start, count)],
                        target.at[pl.ds(row, count), pl.ds(column, 256)],
                        sem,
                    )
                )
        for copy in copies:
            copy.start()
        g_in[...] = jnp.zeros_like(g_in)
        g_down[...] = jnp.zeros_like(g_down)
        for copy in copies:
            copy.wait()

    mine = at_row < pl.num_programs(0) // 2
    ffn = jnp.where(mine, ffn_ref[...], ffn_other_ref[...])
    cot = jnp.where(mine, cot_ref[...], cot_other_ref[...])
    both = dot(ffn, w_in[...], 1, 0)
    grad_hidden = dot(cot, w_down[...], 1, 1)
    gate, upper = both[:, :wide], both[:, wide:]
    sigmoid = 1.0 / (1.0 + jnp.exp(-gate))
    silu = gate * sigmoid
    hidden = (silu * upper).astype(LOW)
    d_gate = (grad_hidden * upper * sigmoid * (1.0 + gate * (1.0 - sigmoid))).astype(LOW)
    d_up = (grad_hidden * silu).astype(LOW)
    d_both = jnp.concatenate([d_gate, d_up], axis=1)
    term = dot(hidden, w_down[...], 1, 0)
    out_ref[...] = term if fresh else out_in[...] + term
    term = dot(d_both, w_in[...], 1, 1)
    back_ref[...] = term if fresh else back_in[...] + term
    g_down[...] += dot(hidden, cot, 0, 0)
    g_in[...] += dot(ffn, d_both, 0, 0)

    @pl.when(at_row == pl.num_programs(0) - 1)
    def _():
        shard = ids_ref[shards]
        for mark in range(shards):
            block = lax.bitwise_xor(shard, jnp.int32(mark))
            for start, count, column, first, base in parts:
                source = g_in if first else g_down
                row = pl.multiple_of(block * count + base, count)
                stage[mark, start : start + count] = source[
                    pl.ds(row, count), column : column + 256
                ].astype(LOW)
        half = stage.shape[1] // 2
        copies = []
        for stream, (_, leave, stay) in enumerate(block_orders(shards.bit_length() - 1)):
            for side, marks in enumerate((leave, stay)):
                for slot, mark in enumerate(marks):
                    copies.append(
                        pltpu.make_async_copy(
                            stage.at[mark, pl.ds(stream * half, half)],
                            sides[2 * stream + side].at[slot],
                            out_sem,
                        )
                    )
        for copy in copies:
            copy.start()
        for copy in copies:
            copy.wait()


def ffn_piece(ids, ffn_pair, cot_pair, blocks, sums, tile=256):
    shards = len(blocks)
    rows = blocks[0].shape[0]
    count, model = ffn_pair[0].shape
    count = 2 * count
    half = count // tile // 2
    wide = shards * rows * 256 // (3 * model)
    fresh = sums is None
    tall = pl.BlockSpec((tile, model), lambda i, ids: (i, 0))
    mine = pl.BlockSpec((tile, model), lambda i, ids: (jnp.minimum(i, half - 1), 0))
    other = pl.BlockSpec((tile, model), lambda i, ids: (jnp.maximum(i - half, 0), 0))
    where = pl.BlockSpec(memory_space=pltpu.HBM)
    sums = () if fresh else tuple(sums)
    side = jax.ShapeDtypeStruct((shards // 2, rows // 2, 256), LOW)
    total = jax.ShapeDtypeStruct((count, model), FULL)
    flops = 18 * count * model * wide
    return pl.pallas_call(
        functools.partial(ffn_kernel, shards=shards, fresh=fresh),
        grid_spec=pltpu.PrefetchScalarGridSpec(
            num_scalar_prefetch=1,
            grid=(count // tile,),
            in_specs=[mine, other] * 2 + [where] * shards + [tall] * len(sums),
            out_specs=[tall, tall] + [where] * 4,
            scratch_shapes=[
                pltpu.VMEM((model, 2 * wide), LOW),
                pltpu.VMEM((wide, model), LOW),
                pltpu.VMEM((model, 2 * wide), FULL),
                pltpu.VMEM((wide, model), FULL),
                pltpu.VMEM((shards, rows, 256), LOW),
                pltpu.SemaphoreType.DMA,
                pltpu.SemaphoreType.DMA,
            ],
        ),
        out_shape=[total, total] + [side] * 4,
        input_output_aliases={} if fresh else {5 + shards: 0, 6 + shards: 1},
        compiler_params=pltpu.CompilerParams(vmem_limit_bytes=60 * 1024 * 1024),
        cost_estimate=pl.CostEstimate(flops=flops, bytes_accessed=40_000_000, transcendentals=0),
        name="ffn_piece",
    )(ids, *ffn_pair, *cot_pair, *blocks, *sums)


def query_blocks(length):
    size = min(256, length)
    for start in range(0, length, size):
        low = max(0, start - DOC_MAX)
        yield start, start + size, low


def attend_kernel(q_ref, k_ref, v_ref, mask_ref, o_ref, log_ref):
    length = q_ref.shape[1]
    value = jnp.concatenate([v_ref[...], jnp.ones((16, length), LOW)], axis=0)
    for group in range(HQ // HK):
        head = slice(group * DH, (group + 1) * DH)
        for start, end, low in query_blocks(length):
            scores = dot(k_ref[:, low:end], q_ref[head, start:end], 0, 0)
            terms = jnp.exp(scores).astype(LOW) * mask_ref[low:end, start:end]
            mixed = dot(value[:, low:end], terms, 1, 0)
            total = mixed[DH : DH + 1]
            o_ref[head, start:end] = (mixed[:DH] * (1.0 / total)).astype(LOW)
            log_ref[0, group : group + 1, start:end] = jnp.log(total)


def attend(q_low, k_low, v_low, mask):
    length = q_low.shape[1]
    wide = HQ // HK * DH
    return pl.pallas_call(
        attend_kernel,
        grid=(HK,),
        in_specs=[
            pl.BlockSpec((wide, length), lambda c: (c, 0)),
            pl.BlockSpec((DH, length), lambda c: (c, 0)),
            pl.BlockSpec((DH, length), lambda c: (c, 0)),
            pl.BlockSpec((length, length), lambda c: (0, 0)),
        ],
        out_specs=[
            pl.BlockSpec((wide, length), lambda c: (c, 0)),
            pl.BlockSpec((1, HQ // HK, length), lambda c: (c, 0, 0)),
        ],
        out_shape=[
            jax.ShapeDtypeStruct((HQ * DH, length), LOW),
            jax.ShapeDtypeStruct((HK, HQ // HK, length), FULL),
        ],
        compiler_params=pltpu.CompilerParams(vmem_limit_bytes=40 * 1024 * 1024),
        cost_estimate=pl.CostEstimate(
            flops=16_000_000_000, bytes_accessed=8_000_000, transcendentals=10_000_000
        ),
        name="attend",
    )(q_low, k_low, v_low, mask)


def row_pair(row, count):
    high = row.astype(LOW).astype(FULL)
    place = lax.broadcasted_iota(jnp.int32, (count, row.shape[1]), 0)
    return jnp.where(place == 0, high, jnp.where(place == 1, row - high, 0.0)).astype(LOW)


def attend_back_kernel(
    q_ref, k_ref, v_ref, o_ref, do_ref, log_ref, mask_ref, dq_ref, dk_ref, dv_ref, value_sum
):
    length = q_ref.shape[1]
    place = lax.broadcasted_iota(jnp.int32, (16, length), 0)
    twos = jnp.where(place < 2, 1.0, 0.0).astype(LOW)
    key = jnp.concatenate([k_ref[...], twos], axis=0)
    value = jnp.concatenate([v_ref[...], twos], axis=0)
    dk_ref[...] = jnp.zeros_like(dk_ref)
    value_sum[...] = jnp.zeros_like(value_sum)
    for group in range(HQ // HK):
        head = slice(group * DH, (group + 1) * DH)
        for start, end, low in query_blocks(length):
            q_blk = q_ref[head, start:end]
            do_blk = do_ref[head, start:end]
            inner = jnp.sum(
                do_blk.astype(FULL) * o_ref[head, start:end].astype(FULL), axis=0, keepdims=True
            )
            log_row = log_ref[0, group : group + 1, start:end]
            q_more = jnp.concatenate([q_blk, row_pair(-log_row, 16)], axis=0)
            do_more = jnp.concatenate([do_blk, row_pair(-inner, 16)], axis=0)
            mask = mask_ref[low:end, start:end]
            probs = jnp.exp(dot(key[:, low:end], q_more, 0, 0))
            grads = dot(value[:, low:end], do_more, 0, 0)
            probs_low = probs.astype(LOW) * mask
            grads_low = (probs * grads).astype(LOW) * mask
            dq_ref[head, start:end] = dot(k_ref[:, low:end], grads_low, 1, 0) * DH ** (-0.5)
            dk_ref[:, low:end] += dot(q_blk, grads_low, 1, 1)
            value_sum[:, low:end] += dot(do_blk, probs_low, 1, 1)
    dv_ref[...] = value_sum[...].astype(LOW)


def attend_back(q_low, k_low, v_low, o_low, do_low, log_total, mask):
    length = q_low.shape[1]
    wide = HQ // HK * DH
    two = pl.BlockSpec((wide, length), lambda c: (c, 0))
    one = pl.BlockSpec((DH, length), lambda c: (c, 0))
    return pl.pallas_call(
        attend_back_kernel,
        grid=(HK,),
        in_specs=[
            two,
            one,
            one,
            two,
            two,
            pl.BlockSpec((1, HQ // HK, length), lambda c: (c, 0, 0)),
            pl.BlockSpec((length, length), lambda c: (0, 0)),
        ],
        out_specs=[two, one, one],
        out_shape=[
            jax.ShapeDtypeStruct((HQ * DH, length), FULL),
            jax.ShapeDtypeStruct((HK * DH, length), FULL),
            jax.ShapeDtypeStruct((HK * DH, length), LOW),
        ],
        scratch_shapes=[pltpu.VMEM((DH, length), FULL)],
        compiler_params=pltpu.CompilerParams(vmem_limit_bytes=40 * 1024 * 1024),
        cost_estimate=pl.CostEstimate(
            flops=40_000_000_000, bytes_accessed=16_000_000, transcendentals=10_000_000
        ),
        name="attend_back",
    )(q_low, k_low, v_low, o_low, do_low, log_total, mask)


def per_device(
    links,
    tokens,
    doc_ids,
    w_query,
    w_key,
    w_value,
    w_out,
    w_gate,
    w_up,
    w_down,
    attn_gain,
    ffn_gain,
    query_gain,
    key_gain,
    cotangent,
):
    shards = links.shards
    _, rep = links.here()
    core = rep & 1
    count, model = tokens.shape
    own = model // shards
    half = own // 2
    kv_wide = HK * DH
    heads_own = DH // shards
    hidden_all = w_gate.shape[1]
    hidden_own = hidden_all // shards
    step = hidden_own // (2 * PIECES)
    packed_wide = model + 2 * kv_wide

    whole_wide = packed_wide + model
    gains = jnp.concatenate([attn_gain, ffn_gain, query_gain, key_gain])
    gains = jnp.pad(gains, (0, whole_wide - gains.shape[0]))[None]
    gains = jnp.pad(gains, ((0, GAIN_ROWS - 1), (0, 0)))
    attn_part = jnp.concatenate(
        [
            lax.dynamic_slice_in_dim(weight, core * half, half, 0)
            for weight in (w_query, w_key, w_value, w_out)
        ],
        axis=1,
    )
    attn_part = jnp.concatenate([attn_part, gains], axis=0)
    ids = links.ids()
    core_line = core[None]
    attn_near = links.near(attn_part)
    held = hold([w_gate, w_up, w_down, cotangent], attn_part)
    cot_pair = [cotangent, links.core_swap(held[3])]
    packed = list(pack(core_line, *held[:3], shards))
    attn_blocks = links.gather(attn_part, attn_near, packed[0], cot_pair[1])
    (packed[0],) = hold([packed[0]], attn_blocks[1])
    nears = [links.near(packed[0])]

    positions = doc_positions(doc_ids).reshape(count)
    freqs = jnp.power(ROPE_BASE, -2.0 * jnp.arange(DH // 2, dtype=FULL) / DH)
    angles = freqs[:, None] * positions.astype(FULL)[None, :]
    cosine, sine = jnp.cos(angles)[None], jnp.sin(angles)[None]
    index = jnp.arange(count)
    doc_row = doc_ids[0]
    mask = (
        (index[:, None] <= index[None, :]) & (doc_row[:, None] == doc_row[None, :])
    ).astype(LOW)

    x_in = tokens.astype(FULL)
    inv_one = inverse_rms(x_in, 1)
    x_hat = x_in * inv_one
    (line,) = hold([ids], nears[0], inv_one, cosine, sine, mask)
    attn_mine = line_up(line, attn_blocks, half)
    attn_full = both_cores(core_line, attn_mine, links.core_swap(attn_mine))
    qkv_full, out_full = attn_full[:, :packed_wide], attn_full[:, packed_wide:]

    gain_rows = jnp.zeros((shards, whole_wide), LOW)
    for place, block in enumerate(attn_blocks):
        gain_rows = lax.dynamic_update_slice(gain_rows, block[half][None], (ids[place], 0))
    gain_rows = gain_rows.astype(FULL)
    gain_attn = gain_rows[:, :own].reshape(model)
    gain_ffn = gain_rows[:, own : 2 * own].reshape(model)
    gain_query = gain_rows[:, 2 * own : 2 * own + heads_own].reshape(1, DH, 1)
    gain_key = gain_rows[:, 2 * own + heads_own : 2 * own + 2 * heads_own].reshape(1, DH, 1)

    attn_in = (x_hat * gain_attn).astype(LOW)
    (attn_in,) = hold([attn_in], nears[0])
    ffn_weights = [links.gather(packed[0], nears[0])]
    (packed[1],) = hold([packed[1]], nears[0])
    nears.append(links.near(packed[1]))
    qkv = dot(qkv_full, attn_in, 0, 1)
    q_heads = qkv[:model].reshape(HQ, DH, count)
    k_heads = qkv[model : model + kv_wide].reshape(HK, DH, count)
    v_low = qkv[model + kv_wide :].astype(LOW)
    q_inv = inverse_rms(q_heads, 1)
    q_hat = q_heads * q_inv
    k_inv = inverse_rms(k_heads, 1)
    k_hat = k_heads * k_inv
    q_low = (rotate(q_hat * gain_query, cosine, sine).astype(LOW) * DH ** (-0.5)).reshape(
        model, count
    )
    k_low = rotate(k_hat * gain_key, cosine, sine).astype(LOW).reshape(kv_wide, count)
    mix_low, log_total = attend(q_low, k_low, v_low, mask)
    (mix_low,) = hold([mix_low], nears[1], *ffn_weights[0])
    ffn_weights.append(links.gather(packed[1], nears[1]))
    for piece in range(2, PIECES):
        (packed[piece],) = hold([packed[piece]], nears[piece - 1])
        nears.append(links.near(packed[piece]))

    resid = x_in + dot(mix_low, out_full, 0, 0)
    inv_two = inverse_rms(resid, 1)
    resid_hat = resid * inv_two
    ffn_in = (resid_hat * gain_ffn).astype(LOW)
    ffn_pair = [ffn_in, links.core_swap(ffn_in)]

    sums, sends = None, []
    ffn_totals = []
    for piece in range(PIECES):
        (order,) = hold([ids], *sends)
        *sums, leave_a, stay_a, leave_b, stay_b = ffn_piece(
            order, ffn_pair, cot_pair, ffn_weights[piece], sums
        )
        if piece + 2 < PIECES:
            ffn_weights.append(links.gather(packed[piece + 2], nears[piece + 2], stay_a))
        sends = []
        for number, entry in enumerate(ffn_totals):
            if piece == PIECES - 1 and number == 0:
                continue
            entry[1] = entry[0].send(stay_a)
            sends += entry[1]
        flow = links.total([leave_a, stay_a, leave_b, stay_b], 0)
        ffn_totals.append([flow, next(flow)])

    out_sum, ffn_back = sums
    first_sent = ffn_totals[0][0].send(stay_a)
    (back_other,) = hold(
        [links.core_swap(ffn_back[count:].astype(LOW))], *first_sent, *sends
    )
    grad_ffn_in = ffn_back[:count] + back_other.astype(FULL)
    grad_gain_ffn = jnp.sum(grad_ffn_in * resid_hat, axis=0)
    grad_resid = cotangent.astype(FULL) + norm_back(grad_ffn_in * gain_ffn, resid_hat, inv_two, 1)
    grad_resid_low = grad_resid.astype(LOW)

    def owned(part):
        theirs = links.core_swap(part)
        low = jnp.where(core == 0, part, theirs)
        high = jnp.where(core == 0, theirs, part)
        return jnp.concatenate([low, high], axis=0).astype(FULL)

    grad_mix = dot(out_full, grad_resid_low, 1, 1).astype(LOW)
    flows = [entry[0] for entry in ffn_totals]
    done = [None] * len(flows)

    def advance(*tokens):
        sent = []
        token = tokens[0] if tokens else None
        for place in reversed(range(len(flows))):
            if done[place] is None:
                got = flows[place].send(token)
                if place >= PIECES and isinstance(got, list):
                    token = got[0]
                if isinstance(got, list):
                    sent += got
                else:
                    done[place] = got
        return sent

    do_low = grad_mix
    dq_rot, dk_rot, dv_low = attend_back(q_low, k_low, v_low, mix_low, do_low, log_total, mask)
    sent = advance(dv_low)
    (dq_rot, dk_rot) = hold([dq_rot, dk_rot], *sent)
    (
        grad_query_w,
        grad_key_w,
        grad_value_w,
        grad_out_w,
        grad_input,
        own_q,
        own_k,
        grad_gain_attn,
    ) = attend_grads(
        dq_rot,
        dk_rot,
        dv_low,
        qkv,
        cosine[0],
        sine[0],
        gain_query[0],
        gain_key[0],
        attn_in,
        attn_full,
        mix_low,
        grad_resid_low,
        tokens,
        inv_one,
        gain_attn[None],
        grad_resid,
    )
    sent = advance(grad_key_w)

    gain_grads = jnp.concatenate(
        [
            grad_gain_attn.reshape(shards, own),
            grad_gain_ffn.reshape(shards, own),
            own_q.reshape(shards, heads_own),
            own_k.reshape(shards, heads_own),
        ],
        axis=1,
    )
    gain_rows = jnp.pad(
        gain_grads.astype(LOW), ((0, 0), (0, whole_wide - gain_grads.shape[1]))
    )[:, None]
    gain_rows = jnp.pad(gain_rows, ((0, 0), (0, GAIN_ROWS - 1), (0, 0)))
    (shard_line,) = hold([jnp.stack([ids[shards], core])], *sent)
    keep, give = sort_out(
        shard_line, [grad_query_w, grad_key_w, grad_value_w, grad_out_w], gain_rows
    )
    came = links.core_swap(give)
    attn_flow = links.total(links.by_mark(add_low(keep, came)), 1, True)
    flows = flows + [attn_flow]
    done = done + [None]
    token = next(attn_flow)[0]
    while None in done[: PIECES - 1]:
        advance(token)
        token = None
    (out_low,) = hold([out_sum[count:].astype(LOW)], done[0])
    out_other = links.core_swap(out_low)
    result = (resid + out_sum[:count] + out_other.astype(FULL)).astype(LOW)
    while done[PIECES - 1] is None:
        token = None
        if links.paired and links.rep_bits == 3:
            attn_flow.send(None)
            attn_flow.send(None)
            token = result
        done[PIECES - 1] = flows[PIECES - 1].send(token)
    ffn_mine = done[:PIECES]
    ffn_theirs = [links.core_swap(part) for part in ffn_mine]
    grad_gate_w, grad_up_w, grad_down_w = unpack(
        core_line, ffn_mine, ffn_theirs, (w_gate.shape, w_up.shape, w_down.shape), shards
    )
    while None in done:
        advance((result, grad_down_w))
    gain_sum = done[-1][half].astype(FULL)
    attn_sum = owned(done[-1][:half])
    ffn_mine = done[:PIECES]
    ffn_theirs = [links.core_swap(part) for part in ffn_mine]
    grad_gate_w, grad_up_w, grad_down_w = unpack(
        core_line, ffn_mine, ffn_theirs, (w_gate.shape, w_up.shape, w_down.shape), shards
    )
    at_value = model + kv_wide
    return (
        result,
        grad_input,
        attn_sum[:, :model],
        attn_sum[:, model:at_value],
        attn_sum[:, at_value:packed_wide],
        attn_sum[:, packed_wide:],
        grad_gate_w,
        grad_up_w,
        grad_down_w,
        gain_sum[:own],
        gain_sum[own : 2 * own],
        gain_sum[2 * own : 2 * own + heads_own],
        gain_sum[2 * own + heads_own : 2 * own + 2 * heads_own],
    )


def solution(mesh):
    both = P(("shard", "rep"), None)
    rows = P("shard", None)
    line = P("shard")
    in_specs = (both, both) + (rows,) * 7 + (line,) * 4 + (both,)
    out_specs = (both, both) + (rows,) * 7 + (line,) * 4
    return jax.shard_map(
        functools.partial(per_device, Links(mesh)),
        mesh=mesh,
        in_specs=in_specs,
        out_specs=out_specs,
        check_vma=False,
    )
```
